128 devices in a mesh: section: 8 (over z, y_hi), dp: 16 (over x, y_lo, core).
Axes of the slice: x: 4, y: 4 (y_hi: 2, y_lo: 2; y = y_hi * 2 + y_lo), z: 4, core: 2. Of those that a mesh axis runs over, the one named last changes fastest.
Arguments:
- incoming: bfloat16 [8, 1024, 4096], P('section', 'dp'), may hold values from -6 to 6
- parked: bfloat16 [8, 1024, 4096], P('section', 'dp'), may hold values from -6 to 6
- cotangent: bfloat16 [8, 1024, 4096], P('section', 'dp'), may hold values from -6 to 6
- norm_gain: float32 [8, 4096], P('section'), may hold values from 0.5 to 1.5
- query_weight: bfloat16 [8, 4096, 4096], P('section', None, 'dp'), may hold values from -2.90625 to 2.90625
- keyval_weight: bfloat16 [8, 4096, 2048], P('section', None, 'dp'), may hold values from -0.09375 to 0.09375
- output_weight: bfloat16 [8, 4096, 4096], P('section', 'dp'), may hold values from -0.09375 to 0.09375
- teacher_id: int32 [1024], P('dp'), may hold values from 0 to 3
- language_id: int32 [1024], P('dp'), may hold values from 0 to 15
Outputs:
- next_input: bfloat16 [8, 1024, 4096], P('section', 'dp')
- input_grad: bfloat16 [8, 1024, 4096], P('section', 'dp')
- parked_next: bfloat16 [8, 1024, 4096], P('section', 'dp')
- query_grad: bfloat16 [8, 4096, 4096], P('section', None, 'dp')
- keyval_grad: bfloat16 [8, 4096, 2048], P('section', None, 'dp')
- output_grad: bfloat16 [8, 4096, 4096], P('section', 'dp')
- gain_grad: float32 [8, 4096], P('section', 'dp')
The draws below stay inside these ranges and needn't reach their ends.
All inputs are finite; a program needn't handle non-finite values.
Results may differ from the reference program's by a relative error of at most 0.024.
Values may be sent and summed in bfloat16 or wider, within the bound.
A program may use at most 192 MiB of HBM per device.

```python
import math
import jax
import jax.numpy as jnp
from jax import lax

D = 4096
HD = 128
HEADS_DEV = 2
TEACHERS = 4
LANGS = 16
HEADS = 32
KVH = 8
SEQ = 1024
SECTIONS = 8
N_DP = 16


def key_columns(key):
    base = jax.random.normal(key, (SECTIONS, D, KVH, HD), jnp.float32)
    return jnp.clip(base, -6.0, 6.0) * D ** (-0.5)


def token_rows(key, share):
    first, second = jax.random.split(key)
    base = jax.random.normal(first, (SECTIONS, SEQ, D), jnp.float32)
    earlier = jnp.roll(base, 1, axis=1)
    position = lax.broadcasted_iota(jnp.int32, (SECTIONS, SEQ, 1), 1)
    picked = jax.random.uniform(second, (SECTIONS, SEQ, 1), jnp.float32) < share
    repeated = jnp.logical_and(picked, position % 2 == 1)
    rows = jnp.where(repeated, earlier, base)
    return jnp.clip(rows, -6.0, 6.0).astype(jnp.bfloat16)


def query_columns(keys, key, lowest, highest):
    first, second, third = jax.random.split(key, 3)
    group = HEADS // KVH
    base = jnp.clip(jax.random.normal(first, (SECTIONS, D, KVH, group, HD), jnp.float32), -6.0, 6.0) * D ** (-0.5)
    chosen = jax.random.randint(second, (SECTIONS, 1, KVH, 1, 1), 0, group)
    member = lax.broadcasted_iota(jnp.int32, (1, 1, 1, group, 1), 3)
    strength = jax.random.uniform(third, (SECTIONS, 1, KVH, 1, 1), jnp.float32, lowest, 1e-06)
    strength = jnp.where(member == chosen, jnp.minimum(strength, highest), 0.0)
    columns = base + strength * keys[:, :, :, None, :]
    return columns.reshape(SECTIONS, D, HEADS * HD).astype(jnp.bfloat16)


def draw_incoming(key, part):
    key = jax.random.fold_in(key, 11)
    return token_rows(key, 0.0)


def draw_parked(key, part):
    key = jax.random.fold_in(key, 12)
    return token_rows(key, 0.0)


def draw_query_weight(key, part):
    keys = key_columns(key)
    key = jax.random.fold_in(key, 22)
    return query_columns(keys, key, 0.0, 0.0)


def draw_keyval_weight(key, part):
    keys = key_columns(key)
    key = jax.random.fold_in(key, 21)
    values = jnp.clip(jax.random.normal(key, (SECTIONS, D, KVH, HD), jnp.float32), -6.0, 6.0) * D ** (-0.5)
    return jnp.stack([keys, values], axis=3).reshape(SECTIONS, D, 2 * KVH * HD).astype(jnp.bfloat16)


def plant(values, own_key, smallest, top_value):
    shape = values.shape
    index_at = [jax.random.randint(jax.random.fold_in(own_key, axis), (), 0, shape[axis]) for axis in range(len(shape))]
    values = values.at[tuple(index_at)].set(smallest)
    longest = shape.index(max(shape))
    index_at[longest] = (index_at[longest] + 1) % shape[longest]
    return values.at[tuple(index_at)].set(top_value)


def steps_of(rng, shape, pieces, least, top_value):
    def one(dim, shards_of):
        draws = jax.random.uniform(jax.random.fold_in(jax.random.fold_in(rng, 6), dim), (shards_of,), jnp.float32, least / len(pieces), top_value / len(pieces))
        return jnp.repeat(jnp.exp(draws), shape[dim] // shards_of).reshape((-1,) + (1,) * (len(shape) - dim - 1))

    factor_of = one(*pieces[0])
    for cut in pieces[1:]:
        factor_of = factor_of * one(*cut)
    return factor_of


def scatter_about(rng, dims, deviation, most, cuts=(), kind=jnp.bfloat16):
    level = steps_of(rng, dims, cuts, -0.22, 0.18) if cuts else 1.0
    entries = jax.random.normal(rng, dims, jnp.float32) * deviation * level
    return jnp.minimum(jnp.maximum(entries, -most), most).astype(kind)


def setup_inputs(seed: int = 0) -> dict:
    key_of = jax.random.split(jax.random.key(seed), 10)
    incoming = draw_incoming(jax.random.fold_in(key_of[9], 71), 0)
    parked = draw_parked(jax.random.fold_in(key_of[9], 71), 0)
    cotangent = scatter_about(key_of[2], (SECTIONS, SEQ, D), 1.0, 6.0, ((0, 8), (1, 16)))
    norm_gain = jnp.clip(1.0 + 0.1 * jax.random.normal(key_of[3], (SECTIONS, D), jnp.float32), 0.5, 1.5)
    query_weight = draw_query_weight(jax.random.fold_in(key_of[9], 71), 0)
    keyval_weight = draw_keyval_weight(jax.random.fold_in(key_of[9], 71), 0)
    output_weight = scatter_about(key_of[6], (SECTIONS, HEADS * HD, D), (HEADS * HD) ** -0.5, 0.09375, ((0, 8), (1, 16)))
    teacher_id = plant(jax.random.randint(key_of[7], (SEQ,), 0, TEACHERS), jax.random.fold_in(key_of[7], 1), 0, TEACHERS - 1).astype(jnp.int32)
    language_id = plant(jax.random.randint(key_of[8], (SEQ,), 0, LANGS), jax.random.fold_in(key_of[8], 1), 0, LANGS - 1).astype(jnp.int32)
    return dict(incoming=incoming, parked=parked, cotangent=cotangent, norm_gain=norm_gain, query_weight=query_weight, keyval_weight=keyval_weight, output_weight=output_weight, teacher_id=teacher_id, language_id=language_id)


EPSILON = 1e-05
NEG_FILL = -1e+30

def normalize(row_block, gain_row):
    values = row_block.astype(jnp.float32)
    inverse_rms = lax.rsqrt(lax.optimization_barrier(jnp.mean(values * values, axis=-1, keepdims=True)) + EPSILON)
    return values * inverse_rms * gain_row

def attend(queries, key_rows, values):
    length = queries.shape[0]
    scores = jnp.einsum('qhd,kd->hqk', queries, key_rows, precision=lax.Precision.HIGHEST) * (1.0 / math.sqrt(key_rows.shape[-1]))
    row_index = lax.broadcasted_iota(jnp.int32, (length, length), 0)
    col_index = lax.broadcasted_iota(jnp.int32, (length, length), 1)
    scores = jnp.where((col_index <= row_index)[None], scores, NEG_FILL)
    row_max = lax.stop_gradient(lax.optimization_barrier(jnp.max(scores, axis=-1, keepdims=True)))
    weights = jnp.exp(scores - row_max)
    weights = weights / lax.optimization_barrier(jnp.sum(weights, axis=-1, keepdims=True))
    return jnp.einsum('hqk,kd->qhd', weights, values, precision=lax.Precision.HIGHEST)

def attend_all(head_queries, key_rows, values):
    return jax.vmap(attend, in_axes=(1, 1, 1), out_axes=1)(head_queries, key_rows, values)

def project(normed, weight_query, weight_keyval):
    queries = jnp.dot(normed, weight_query, preferred_element_type=jnp.float32).astype(jnp.bfloat16)
    keyval = jnp.dot(normed, weight_keyval, preferred_element_type=jnp.float32).astype(jnp.bfloat16)
    return (queries, keyval)

def split_heads(queries, keyval, group_size):
    length = queries.shape[0]
    head_queries = queries.astype(jnp.float32).reshape(length, KVH, group_size, HD)
    paired = keyval.astype(jnp.float32).reshape(length, KVH, 2, HD)
    return (head_queries, paired[:, :, 0], paired[:, :, 1])

def rounded_term(term):
    return lax.optimization_barrier(term.astype(jnp.bfloat16)).astype(jnp.float32)

def forward_groups(attended, weight_output):
    width = HEADS_DEV * HD

    def add_group(index, total):
        start = (index * width).astype(jnp.int32)
        left = lax.dynamic_slice_in_dim(attended, start, width, 1)
        right = lax.dynamic_slice_in_dim(weight_output, start, width, 0)
        return total + rounded_term(jnp.dot(left, right, preferred_element_type=jnp.float32))
    return lax.fori_loop(0, N_DP, add_group, jnp.zeros((attended.shape[0], weight_output.shape[1]), jnp.float32))

def backward_groups(d_queries, d_keyval, weight_query, weight_keyval):
    width = HEADS_DEV * HD

    def add_group(index, total):
        query_start = (index * width).astype(jnp.int32)
        keyval_start = (index * HD).astype(jnp.int32)
        query_block = lax.dynamic_slice_in_dim(d_queries, query_start, width, 1)
        query_cols = lax.dynamic_slice_in_dim(weight_query, query_start, width, 1)
        keyval_block = lax.dynamic_slice_in_dim(d_keyval, keyval_start, HD, 1)
        keyval_cols = lax.dynamic_slice_in_dim(weight_keyval, keyval_start, HD, 1)
        term = jnp.dot(query_block, query_cols.T, preferred_element_type=jnp.float32)
        term = term + jnp.dot(keyval_block, keyval_cols.T, preferred_element_type=jnp.float32)
        return total + rounded_term(term)
    return lax.fori_loop(0, N_DP, add_group, jnp.zeros((d_queries.shape[0], weight_query.shape[0]), jnp.float32))

def reference(incoming, parked, cotangent, norm_gain, query_weight, keyval_weight, output_weight, teacher_id, language_id):
    group_size = HEADS // KVH
    token_weight = jnp.power(0.5, teacher_id.astype(jnp.float32)) * (0.5 + language_id.astype(jnp.float32) / (LANGS - 1))
    forward_list = []
    back_list = []
    query_list = []
    keyval_list = []
    output_list = []
    gain_list = []
    for section_id in range(SECTIONS):
        gain_row = norm_gain[section_id]
        row_block = incoming[section_id]
        normed = normalize(row_block, gain_row).astype(jnp.bfloat16)
        queries, keyval = project(normed, query_weight[section_id], keyval_weight[section_id])
        head_queries, key_rows, values = split_heads(queries, keyval, group_size)
        attended = attend_all(head_queries, key_rows, values).reshape(SEQ, HEADS * HD).astype(jnp.bfloat16)
        combined = row_block.astype(jnp.float32) + forward_groups(attended, output_weight[section_id])
        forward_list.append(combined.astype(jnp.bfloat16))
        stash_rows = parked[(section_id + SECTIONS // 2) % SECTIONS]
        normed_f, undo_norm = jax.vjp(normalize, stash_rows.astype(jnp.float32), gain_row)
        normed_b = normed_f.astype(jnp.bfloat16)
        queries_b, keyval_b = project(normed_b, query_weight[section_id], keyval_weight[section_id])
        head_queries, key_rows, values = split_heads(queries_b, keyval_b, group_size)
        attended_f, undo_attend = jax.vjp(attend_all, head_queries, key_rows, values)
        attended_b = attended_f.reshape(SEQ, HEADS * HD).astype(jnp.bfloat16)
        upstream = cotangent[section_id]
        if section_id == SECTIONS - 1:
            upstream = (upstream.astype(jnp.float32) * token_weight[:, None]).astype(jnp.bfloat16)
        output_list.append(jnp.dot(attended_b.T, upstream, preferred_element_type=jnp.float32).astype(jnp.bfloat16))
        d_attended = jnp.dot(upstream, output_weight[section_id].T, preferred_element_type=jnp.float32)
        d_heads, d_keys, d_values = undo_attend(d_attended.reshape(SEQ, KVH, group_size, HD))
        d_queries = d_heads.reshape(SEQ, HEADS * HD).astype(jnp.bfloat16)
        d_keyval = jnp.stack([d_keys, d_values], axis=2).reshape(SEQ, 2 * KVH * HD).astype(jnp.bfloat16)
        query_list.append(jnp.dot(normed_b.T, d_queries, preferred_element_type=jnp.float32).astype(jnp.bfloat16))
        keyval_list.append(jnp.dot(normed_b.T, d_keyval, preferred_element_type=jnp.float32).astype(jnp.bfloat16))
        d_normed = backward_groups(d_queries, d_keyval, query_weight[section_id], keyval_weight[section_id])
        d_rows, d_gain = undo_norm(d_normed)
        gain_list.append(d_gain)
        back_list.append((upstream.astype(jnp.float32) + d_rows).astype(jnp.bfloat16))
    next_input = jnp.roll(jnp.stack(forward_list), 1, axis=0)
    input_grad = jnp.roll(jnp.stack(back_list), -1, axis=0)
    parked_next = jnp.roll(incoming, -(SECTIONS // 2), axis=0)
    return (next_input, input_grad, parked_next, jnp.stack(query_list), jnp.stack(keyval_list), jnp.stack(output_list), jnp.stack(gain_list))
```

```python
import functools
import math

import jax
import jax.numpy as jnp
from jax import lax
from jax.experimental import pallas as pl
from jax.experimental.pallas import tpu as pltpu
from jax.sharding import PartitionSpec as P

LANGS = 16
EPSILON = 1e-05
NEG_FILL = -1e30
MESH = pl.DeviceIdType.MESH
BF16 = jnp.bfloat16
F32 = jnp.float32

SHARD = 64
A, A0, A1 = (0, 32), (0, 16), (16, 16)
B, B0, B1 = (32, 32), (32, 16), (48, 16)
WHOLE = (0, 64)
PLACES = [(0, 0), (0, 1), (-1, 0), (1, 0), (2, 0), (-1, 1), (1, 1), (2, 1)]


def dot(a, b, dims=((1,), (0,))):
    return lax.dot_general(a, b, (dims, ((), ())), preferred_element_type=F32)


class Place:
    def __init__(self):
        self.s = lax.axis_index("section")
        self.d = lax.axis_index("dp")
        self.x = self.d // 4
        self.y = lax.rem(self.d // 2, 2)
        self.c = lax.rem(self.d, 2)

    def index(self, dx, dy, flip=0):
        x = lax.rem(self.x + dx + 4, 4)
        y = self.y if dy == 0 else 1 - self.y
        c = self.c if flip == 0 else 1 - self.c
        return x * 4 + y * 2 + c

    def row(self, dx, dy, part, flip=0):
        start = self.index(dx, dy, flip) * SHARD + part[0]
        return pl.ds(pl.multiple_of(start, 16), part[1])

    def peer(self, dx, dy, flip=0):
        return (self.s, self.index(dx, dy, flip))

    def relay(self, steps):
        return (lax.rem(self.s + steps + 8, 8), self.d)


class Mover:
    def __init__(self, send_sem, recv_sem):
        self.send_sem, self.recv_sem = send_sem, recv_sem
        self.open = []

    def send(self, key, src, dst, target):
        copy = pltpu.make_async_remote_copy(
            src_ref=src, dst_ref=dst, send_sem=self.send_sem.at[key], recv_sem=self.recv_sem.at[key],
            device_id=target, device_id_type=MESH,
        )
        copy.start()
        self.open.append(copy)

    def take(self, key, dst, source):
        pltpu.make_async_remote_copy(
            src_ref=dst, dst_ref=dst, send_sem=self.send_sem.at[key], recv_sem=self.recv_sem.at[key],
            device_id=source, device_id_type=MESH,
        ).wait_recv()

    def drain(self):
        for copy in self.open:
            copy.wait_send()
        self.open = []


class Gather:
    def __init__(self, place, buf, send_sem, recv_sem):
        self.at, self.buf = place, buf
        self.move = Mover(send_sem, recv_sem)

    def go(self, key, where, part, to):
        rows = self.buf.at[self.at.row(*where, part)]
        self.move.send(key, rows, rows, self.at.peer(*to))

    def sib(self, where, part):
        key = 18 + 2 * PLACES.index(where) + (0 if part == A else 1)
        rows = self.buf.at[self.at.row(*where, part)]
        self.move.send(key, rows, rows, self.at.peer(0, 0, 1))

    def got(self, key, where, part):
        self.move.take(key, self.buf.at[self.at.row(*where, part)], self.at.peer(0, 1))

    def start(self):
        own, right, left, up = (0, 0), (1, 0), (-1, 0), (0, 1)
        self.go(13, own, B, up)
        self.go(0, own, A, right)
        self.go(6, own, A, left)
        self.go(12, own, A, up)
        self.go(1, own, B, right)
        self.go(7, own, B, left)
        self.sib(own, A)
        self.sib(own, B)

    def mid(self):
        right, left, up = (1, 0), (-1, 0), (0, 1)
        self.got(13, up, B)
        self.go(2, up, B, right)
        self.go(8, up, B, left)
        self.got(0, left, A)
        self.go(3, left, A0, right)
        self.go(14, left, A, up)
        self.got(6, right, A)
        self.go(9, right, A1, left)
        self.go(15, right, A, up)
        self.sib(up, B)
        self.sib(left, A)
        self.sib(right, A)
        self.got(1, left, B)
        self.go(4, left, B0, right)
        self.got(7, right, B)
        self.go(10, right, B1, left)
        self.sib(left, B)
        self.sib(right, B)

    def mid2(self):
        right, left, up = (1, 0), (-1, 0), (0, 1)
        self.got(2, (-1, 1), B)
        self.go(5, (-1, 1), B0, right)
        self.got(8, (1, 1), B)
        self.go(11, (1, 1), B1, left)
        self.sib((-1, 1), B)
        self.sib((1, 1), B)
        self.got(3, (2, 0), A0)
        self.got(9, (2, 0), A1)
        self.go(16, (2, 0), A, up)
        self.sib((2, 0), A)

    def fin(self):
        self.got(12, (0, 1), A)
        self.sib((0, 1), A)
        self.got(14, (-1, 1), A)
        self.sib((-1, 1), A)
        self.got(15, (1, 1), A)
        self.sib((1, 1), A)
        self.got(4, (2, 0), B0)
        self.got(10, (2, 0), B1)
        self.sib((2, 0), B)
        self.got(5, (2, 1), B0)
        self.got(11, (2, 1), B1)
        self.sib((2, 1), B)
        self.got(16, (2, 1), A)
        self.sib((2, 1), A)
        for i, where in enumerate(PLACES):
            for j, part in enumerate((A, B)):
                self.move.take(18 + 2 * i + j, self.buf.at[self.at.row(*where, part, 1)], self.at.peer(0, 0, 1))


SIZES = [16, 16, 16, 32, 32, 32, 16, 16, 16, 32, 32, 32, 32, 32, 32, 32, 32] + [64] * 8
OFFSETS = [sum(SIZES[:i]) for i in range(len(SIZES))]


class Scatter:
    ORDER = [2, 1, -1, 0]

    def __init__(self, place, buf, land, send_sem, recv_sem):
        self.at, self.buf, self.land = place, buf, land
        self.move = Mover(send_sem, recv_sem)

    def slot(self, key):
        return self.land.at[pl.ds(OFFSETS[key], SIZES[key])]

    def go(self, key, where, part, to):
        self.move.send(key, self.buf.at[self.at.row(*where, part)], self.slot(key), self.at.peer(*to))

    def add(self, key, where, part):
        self.move.take(key, self.slot(key), self.at.peer(0, 1))
        rows = self.at.row(*where, part)
        total = self.buf[rows, :].astype(F32) + self.slot(key)[...].astype(F32)
        self.buf[rows, :] = total.astype(BF16)

    def block(self, dx):
        return pl.multiple_of(lax.rem(self.at.x + dx + 4, 4) * 256, 256)

    def share(self, dx):
        for dy in (1, 0):
            key = 17 + 2 * self.ORDER.index(dx) + dy
            rows = self.buf.at[self.at.row(dx, dy, WHOLE, 1)]
            self.move.send(key, rows, self.slot(key), self.at.peer(0, 0, 1))

    def join(self, dx):
        right, left, up = (1, 0), (-1, 0), (0, 1)
        for dy in (1, 0):
            self.add(17 + 2 * self.ORDER.index(dx) + dy, (dx, dy), WHOLE)
        if dx == 2:
            self.go(0, (2, 1), B0, left)
            self.go(6, (2, 1), B1, right)
            self.go(12, (2, 1), A, up)
            self.go(1, (2, 0), B0, left)
            self.go(7, (2, 0), B1, right)
        else:
            self.go({-1: 13, 1: 14, 0: 15}[dx], (dx, 1), A, up)

    def cross(self):
        right, left = (1, 0), (-1, 0)
        self.add(12, (2, 0), A)
        self.go(2, (2, 0), A0, left)
        self.go(8, (2, 0), A1, right)
        self.add(0, (-1, 1), B0)
        self.go(3, (-1, 1), B, left)
        self.add(6, (1, 1), B1)
        self.go(9, (1, 1), B, right)
        self.add(1, (-1, 0), B0)
        self.go(4, (-1, 0), B, left)
        self.add(7, (1, 0), B1)
        self.go(10, (1, 0), B, right)

    def cross2(self):
        right, left, up = (1, 0), (-1, 0), (0, 1)
        self.add(13, (-1, 0), A)
        self.add(2, (-1, 0), A0)
        self.go(5, (-1, 0), A, left)
        self.add(14, (1, 0), A)
        self.add(8, (1, 0), A1)
        self.go(11, (1, 0), A, right)
        self.add(3, (0, 1), B)
        self.add(9, (0, 1), B)
        self.go(16, (0, 1), B, up)

    def total(self, part):
        keys = (15, 5, 11) if part == A else (4, 10, 16)
        out = self.buf[self.at.row(0, 0, part), :].astype(F32)
        for key in keys:
            self.move.take(key, self.slot(key), self.at.peer(0, 1))
            out = out + self.slot(key)[...].astype(F32)
        return out


def softmax_block(q_blk, keys, first):
    rows, length = q_blk.shape[0], keys.shape[0]
    scale = 1.0 / math.sqrt(q_blk.shape[1])
    scores = dot(q_blk, keys, ((1,), (1,)))
    row_index = lax.broadcasted_iota(jnp.int32, (rows, length), 0) + first
    col_index = lax.broadcasted_iota(jnp.int32, (rows, length), 1)
    scores = jnp.where(col_index <= row_index, scores, NEG_FILL)
    weights = jnp.exp((scores - jnp.max(scores, axis=-1, keepdims=True)) * scale)
    return weights, jnp.sum(weights, axis=-1, keepdims=True)


def kernel(
    inc, parked, cot, gain, tw, wq_hbm, wkv_hbm, wo_hbm,
    next_out, back_out, parkn_out, qg_out, kg_out, og_out, dgain_out,
    g, land, wq, wkv, wo, stash, fwd_rows, back_rows, q, kv, att, d_out, dq, dk, dv, dkv_send, dkv_recv, dkv,
    ag_send, ag_recv, rs_send, rs_recv, misc_send, misc_recv, local_sem,
):
    at = Place()
    length = g.shape[1]
    blocks = length // 256

    barrier = pltpu.get_barrier_semaphore()
    peers = [at.peer(1, 0), at.peer(-1, 0), at.peer(0, 1), at.peer(0, 0, 1), at.relay(4), at.relay(1), at.relay(-1)]
    for peer in peers:
        pl.semaphore_signal(barrier, inc=1, device_id=peer, device_id_type=MESH)
    loads = [
        pltpu.make_async_copy(src, dst, local_sem.at[i])
        for i, (src, dst) in enumerate(((wq_hbm, wq), (wkv_hbm, wkv), (wo_hbm, wo)))
    ]
    for load in loads:
        load.start()

    own = at.row(0, 0, WHOLE)

    def inverse_rms(values):
        return lax.rsqrt(jnp.mean(values * values, axis=-1, keepdims=True) + EPSILON)

    values = inc[...].astype(F32)
    g[0, own, :] = (values * inverse_rms(values) * gain[...]).astype(BF16)
    g[1, own, :] = (cot[...].astype(F32) * tw[...]).astype(BF16)

    pl.semaphore_wait(barrier, len(peers))
    misc = Mover(misc_send, misc_recv)
    misc.send(0, parked, stash, at.relay(4))
    ag = [Gather(at, g.at[i], ag_send.at[i], ag_recv.at[i]) for i in range(3)]
    ag[0].start()
    ag[1].start()
    misc.send(1, inc, parkn_out, at.relay(4))
    ag[0].mid()

    misc.take(0, stash, at.relay(4))
    values = stash[...].astype(F32)
    g[2, own, :] = (values * inverse_rms(values) * gain[...]).astype(BF16)
    ag[2].start()
    ag[0].mid2()
    ag[1].mid()
    ag[0].fin()
    loads[0].wait()
    loads[1].wait()
    core = at.c

    def project(source, slot):
        def step(i, carry):
            rows = pl.ds(pl.multiple_of(i * 256, 256), 256)
            piece = g[source, rows, :]
            q[slot, rows, :] = dot(piece, wq[...]).astype(BF16)
            kv[slot, core, rows, :] = dot(piece, wkv[...]).astype(BF16)
            return carry

        lax.fori_loop(0, blocks, step, 0)
        misc.send(2 + slot, kv.at[slot, core], kv.at[slot, core], at.peer(0, 0, 1))

    def keyval_arrived(slot):
        misc.take(2 + slot, kv.at[slot, 1 - core], at.peer(0, 0, 1))

    project(0, 0)
    ag[1].mid2()
    ag[2].mid()
    keyval_arrived(0)

    def attend(head, carry):
        cols = pl.ds(pl.multiple_of(head * 128, 128), 128)
        for i in range(blocks):
            rows, seen = pl.ds(i * 256, 256), pl.ds(0, (i + 1) * 256)
            weights, norm = softmax_block(q[0, rows, cols], kv[0, 0, seen, :], i * 256)
            att[0, rows, cols] = (dot(weights.astype(BF16), kv[0, 1, seen, :]) / norm).astype(BF16)
        return carry

    lax.fori_loop(0, 2, attend, 0)
    ag[1].fin()
    ag[2].mid2()
    loads[2].wait()
    ag[0].move.drain()

    rs = [Scatter(at, g.at[i], land.at[i], rs_send.at[i], rs_recv.at[i]) for i in range(2)]

    def produce_forward(dx):
        rows = pl.ds(rs[0].block(dx), 256)
        piece = att[0, rows, :]

        def step(j, carry):
            cols = pl.ds(pl.multiple_of(j * 512, 512), 512)
            g[0, rows, cols] = dot(piece, wo[:, cols]).astype(BF16)
            return carry

        lax.fori_loop(0, g.shape[2] // 512, step, 0)
        rs[0].share(dx)

    for dx in Scatter.ORDER:
        produce_forward(dx)

    def cotangent_step(i, carry):
        rows = pl.ds(pl.multiple_of(i * 256, 256), 256)
        d_out[rows, :] = dot(g[1, rows, :], wo[...], ((1,), (1,))).astype(BF16)
        return carry

    lax.fori_loop(0, blocks, cotangent_step, 0)
    ag[2].fin()
    for dx in Scatter.ORDER:
        rs[0].join(dx)
    project(2, 1)
    keyval_arrived(1)
    rs[0].cross()

    dk[...] = jnp.zeros_like(dk)
    dv[...] = jnp.zeros_like(dv)
    scale = 1.0 / math.sqrt(dk.shape[1])

    def attend_back(head):
        cols = pl.ds(head * 128, 128)
        for i in range(blocks):
            rows, seen = pl.ds(i * 256, 256), pl.ds(0, (i + 1) * 256)
            q_blk, keys, vals = q[1, rows, cols], kv[1, 0, seen, :], kv[1, 1, seen, :]
            weights, norm = softmax_block(q_blk, keys, i * 256)
            weights = weights / norm
            rounded = weights.astype(BF16)
            att[1, rows, cols] = dot(rounded, vals).astype(BF16)
            d_blk = d_out[rows, cols]
            d_weights = dot(d_blk, vals, ((1,), (1,)))
            delta = jnp.sum(weights * d_weights, axis=-1, keepdims=True)
            d_scores = (weights * (d_weights - delta) * scale).astype(BF16)
            dq[rows, cols] = dot(d_scores, keys).astype(BF16)
            dk[seen, :] += dot(d_scores, q_blk, ((0,), (0,)))
            dv[seen, :] += dot(rounded, d_blk, ((0,), (0,)))

    attend_back(0)
    rs[0].cross2()
    attend_back(1)
    even = core == 0
    dkv_send[...] = jnp.where(even, dv[...], dk[...]).astype(BF16)
    misc.send(4, dkv_send, dkv_recv, at.peer(0, 0, 1))

    att_t = att[1].T

    def output_grad_step(j, carry):
        cols = pl.ds(pl.multiple_of(j * 512, 512), 512)
        wo[:, cols] = dot(att_t, g[1, :, cols]).astype(BF16)
        return carry

    lax.fori_loop(0, g.shape[2] // 512, output_grad_step, 0)
    og_copy = pltpu.make_async_copy(wo, og_out, local_sem.at[3])
    og_copy.start()

    misc.take(4, dkv_recv, at.peer(0, 0, 1))
    dkv[...] = (jnp.where(even, dk[...], dv[...]) + dkv_recv[...].astype(F32)).astype(BF16)
    ag[1].move.drain()

    def produce_back(dx):
        rows = pl.ds(rs[1].block(dx), 256)
        dq_blk, dkv_blk = dq[rows, :], dkv[rows, :]

        def step(j, carry):
            cols = pl.ds(pl.multiple_of(j * 512, 512), 512)
            term = dot(dq_blk, wq[cols, :], ((1,), (1,))) + dot(dkv_blk, wkv[cols, :], ((1,), (1,)))
            g[1, rows, cols] = term.astype(BF16)
            return carry

        lax.fori_loop(0, g.shape[2] // 512, step, 0)
        rs[1].share(dx)

    produce_back(2)
    produce_back(1)
    rs[1].join(2)
    produce_back(-1)
    rs[1].join(1)
    produce_back(0)
    rs[1].join(-1)
    rs[1].join(0)

    for part in (A, B):
        rows = pl.ds(*part)
        fwd_rows[rows, :] = (inc[rows, :].astype(F32) + rs[0].total(part)).astype(BF16)
    misc.send(5, fwd_rows, next_out, at.relay(1))
    rs[1].cross()

    grad_t = jnp.concatenate([dq[...], dkv[...]], axis=1).T

    def weight_grad_step(j, carry):
        cols = pl.ds(pl.multiple_of(j * 512, 512), 512)
        piece = dot(grad_t, g[2, :, cols]).astype(BF16).T
        wq[cols, :] = piece[:, :256]
        wkv[cols, :] = piece[:, 256:]
        return carry

    half = g.shape[2] // 1024
    lax.fori_loop(0, half, weight_grad_step, 0)
    rs[1].cross2()
    lax.fori_loop(half, 2 * half, weight_grad_step, 0)
    qg_copy = pltpu.make_async_copy(wq, qg_out, local_sem.at[4])
    kg_copy = pltpu.make_async_copy(wkv, kg_out, local_sem.at[5])
    qg_copy.start()
    kg_copy.start()

    d_gain = jnp.zeros((1, g.shape[2]), F32)
    for part in (A, B):
        rows = pl.ds(*part)
        d_normed = rs[1].total(part)
        values = stash[rows, :].astype(F32)
        inverse = inverse_rms(values)
        d_gain = d_gain + jnp.sum(d_normed * (values * inverse), axis=0, keepdims=True)
        scaled = d_normed * gain[...]
        inner = jnp.mean(scaled * values, axis=-1, keepdims=True)
        d_rows = inverse * scaled - values * (inverse * inverse * inverse * inner)
        upstream = (cot[rows, :].astype(F32) * tw[rows, :]).astype(BF16).astype(F32)
        back_rows[rows, :] = (upstream + d_rows).astype(BF16)
    misc.send(6, back_rows, back_out, at.relay(-1))
    dgain_out[...] = d_gain

    for copy in (og_copy, qg_copy, kg_copy):
        copy.wait()
    for mover in (ag[2].move, rs[0].move, rs[1].move):
        mover.drain()
    misc.take(1, parkn_out, at.relay(4))
    misc.take(5, next_out, at.relay(-1))
    misc.take(6, back_out, at.relay(1))
    misc.drain()


def cycle(inc, parked, cot, gain, tw, wq, wkv, wo):
    tokens, width = inc.shape
    length = tokens * lax.axis_size("dp")
    any_spec = pl.BlockSpec(memory_space=pl.ANY)
    vmem_spec = pl.BlockSpec(memory_space=pltpu.VMEM)
    block = jax.ShapeDtypeStruct((tokens, width), BF16)
    shapes = [block, block, block] + [jax.ShapeDtypeStruct(w.shape, BF16) for w in (wq, wkv, wo)]
    shapes.append(jax.ShapeDtypeStruct((1, width), F32))
    heads_width, head_dim = wq.shape[1], wkv.shape[1]
    scratch = [
        pltpu.VMEM((3, length, width), BF16),
        pltpu.VMEM((2, sum(SIZES), width), BF16),
        pltpu.VMEM(wq.shape, BF16),
        pltpu.VMEM(wkv.shape, BF16),
        pltpu.VMEM(wo.shape, BF16),
        pltpu.VMEM((tokens, width), BF16),
        pltpu.VMEM((tokens, width), BF16),
        pltpu.VMEM((tokens, width), BF16),
        pltpu.VMEM((2, length, heads_width), BF16),
        pltpu.VMEM((2, 2, length, head_dim), BF16),
        pltpu.VMEM((2, length, heads_width), BF16),
        pltpu.VMEM((length, heads_width), BF16),
        pltpu.VMEM((length, heads_width), BF16),
        pltpu.VMEM((length, head_dim), F32),
        pltpu.VMEM((length, head_dim), F32),
        pltpu.VMEM((length, head_dim), BF16),
        pltpu.VMEM((length, head_dim), BF16),
        pltpu.VMEM((length, head_dim), BF16),
        pltpu.SemaphoreType.DMA((3, 34)),
        pltpu.SemaphoreType.DMA((3, 34)),
        pltpu.SemaphoreType.DMA((2, 25)),
        pltpu.SemaphoreType.DMA((2, 25)),
        pltpu.SemaphoreType.DMA((7,)),
        pltpu.SemaphoreType.DMA((7,)),
        pltpu.SemaphoreType.DMA((6,)),
    ]
    return pl.pallas_call(
        kernel,
        out_shape=shapes,
        in_specs=[vmem_spec, any_spec, vmem_spec, vmem_spec, vmem_spec, any_spec, any_spec, any_spec],
        out_specs=[any_spec] * 6 + [vmem_spec],
        scratch_shapes=scratch,
        compiler_params=pltpu.CompilerParams(
            collective_id=0, has_side_effects=True, vmem_limit_bytes=60 * 2**20
        ),
        cost_estimate=pl.CostEstimate(flops=24 * 10**9, bytes_accessed=2 * 10**7, transcendentals=4 * 10**6),
        name="relay_cycle",
    )(inc, parked, cot, gain, tw, wq, wkv, wo)


def body(
    incoming,
    parked,
    cotangent,
    norm_gain,
    query_weight,
    keyval_weight,
    output_weight,
    teacher_id,
    language_id,
):
    sections = lax.axis_size("section")
    section_rank = lax.axis_index("section")
    token_weight = jnp.power(0.5, teacher_id.astype(F32)) * (0.5 + language_id.astype(F32) / (LANGS - 1))
    token_weight = jnp.where(section_rank == sections - 1, token_weight, 1.0)[:, None]
    next_input, input_grad, parked_next, query_grad, keyval_grad, output_grad, d_gain = cycle(
        incoming[0], parked[0], cotangent[0], norm_gain, token_weight,
        query_weight[0], keyval_weight[0], output_weight[0],
    )
    ranks = lax.axis_size("dp")
    parts = lax.all_to_all(d_gain.reshape(ranks, -1), "dp", 0, 0)
    gain_grad = jnp.sum(parts, axis=0)
    return tuple(
        item[None]
        for item in (next_input, input_grad, parked_next, query_grad, keyval_grad, output_grad, gain_grad)
    )


def solution(mesh):
    return jax.shard_map(
        body,
        mesh=mesh,
        in_specs=(
            P("section", "dp", None),
            P("section", "dp", None),
            P("section", "dp", None),
            P("section", None),
            P("section", None, "dp"),
            P("section", None, "dp"),
            P("section", "dp", None),
            P("dp"),
            P("dp"),
        ),
        out_specs=(
            P("section", "dp", None),
            P("section", "dp", None),
            P("section", "dp", None),
            P("section", None, "dp"),
            P("section", None, "dp"),
            P("section", "dp", None),
            P("section", "dp"),
        ),
        check_vma=False,
    )
```

```python
import functools
import math

import jax
import jax.numpy as jnp
from jax import lax
from jax.experimental import pallas as pl
from jax.experimental.pallas import tpu as pltpu
from jax.sharding import PartitionSpec as P

LANGS = 16
EPSILON = 1e-05
NEG_FILL = -1e30
MESH = pl.DeviceIdType.MESH
BF16 = jnp.bfloat16
F32 = jnp.float32

SHARD = 64
WHOLE = (0, 64)
PLACES = [(0, 0), (0, 1), (-1, 0), (1, 0), (2, 0), (-1, 1), (1, 1), (2, 1)]


def dot(a, b, dims=((1,), (0,))):
    return lax.dot_general(a, b, (dims, ((), ())), preferred_element_type=F32)


class Split:
    def __init__(self, low, a_cut, middle, b_cut, high):
        self.whole = (low, high - low)
        self.A, self.A0, self.A1 = (low, middle - low), (low, a_cut - low), (a_cut, middle - a_cut)
        self.B, self.B0, self.B1 = (middle, high - middle), (middle, b_cut - middle), (b_cut, high - b_cut)


EVEN = Split(0, 16, 32, 48, 64)
TILT_RIGHT = Split(0, 16, 16, 32, 64)
TILT_LEFT = Split(0, 0, 16, 48, 64)
UPPER = Split(0, 16, 16, 16, 32)
LOWER = Split(32, 32, 48, 64, 64)


class Place:
    def __init__(self):
        self.s = lax.axis_index("section")
        self.d = lax.axis_index("dp")
        self.x = self.d // 4
        self.y = lax.rem(self.d // 2, 2)
        self.c = lax.rem(self.d, 2)

    def index(self, dx, dy, flip=0):
        x = lax.rem(self.x + dx + 4, 4)
        y = self.y if dy == 0 else 1 - self.y
        c = self.c if flip == 0 else 1 - self.c
        return x * 4 + y * 2 + c

    def row(self, dx, dy, part, flip=0):
        start = self.index(dx, dy, flip) * SHARD + part[0]
        return pl.ds(pl.multiple_of(start, 16), part[1])

    def peer(self, dx, dy, flip=0):
        return (self.s, self.index(dx, dy, flip))

    def relay(self, steps):
        return (lax.rem(self.s + steps + 8, 8), self.d)


class Mover:
    def __init__(self, send_sem, recv_sem):
        self.send_sem, self.recv_sem = send_sem, recv_sem
        self.open = []

    def send(self, key, src, dst, target):
        copy = pltpu.make_async_remote_copy(
            src_ref=src, dst_ref=dst, send_sem=self.send_sem.at[key], recv_sem=self.recv_sem.at[key],
            device_id=target, device_id_type=MESH,
        )
        copy.start()
        self.open.append(copy)

    def take(self, key, dst, source):
        pltpu.make_async_remote_copy(
            src_ref=dst, dst_ref=dst, send_sem=self.send_sem.at[key], recv_sem=self.recv_sem.at[key],
            device_id=source, device_id_type=MESH,
        ).wait_recv()

    def drain(self):
        for copy in self.open:
            copy.wait_send()
        self.open = []


class Gather:
    def __init__(self, place, split, buf, send_sem, recv_sem):
        self.at, self.split, self.buf = place, split, buf
        self.move = Mover(send_sem, recv_sem)

    def go(self, key, where, part, to):
        if part[1]:
            rows = self.buf.at[self.at.row(*where, part)]
            self.move.send(key, rows, rows, self.at.peer(*to))

    def sib(self, where, part):
        key = 18 + 2 * PLACES.index(where) + (0 if part == self.split.A else 1)
        rows = self.buf.at[self.at.row(*where, part)]
        self.move.send(key, rows, rows, self.at.peer(0, 0, 1))

    def got(self, key, where, part):
        if part[1]:
            self.move.take(key, self.buf.at[self.at.row(*where, part)], self.at.peer(0, 1))

    def start(self):
        own, right, left, up = (0, 0), (1, 0), (-1, 0), (0, 1)
        self.go(13, own, self.split.B, up)
        self.go(0, own, self.split.A, right)
        self.go(6, own, self.split.A, left)
        self.go(12, own, self.split.A, up)
        self.go(1, own, self.split.B, right)
        self.go(7, own, self.split.B, left)
        self.sib(own, self.split.A)
        self.sib(own, self.split.B)

    def mid(self):
        right, left, up = (1, 0), (-1, 0), (0, 1)
        self.got(13, up, self.split.B)
        self.go(2, up, self.split.B, right)
        self.go(8, up, self.split.B, left)
        self.got(0, left, self.split.A)
        self.go(3, left, self.split.A0, right)
        self.go(14, left, self.split.A, up)
        self.got(6, right, self.split.A)
        self.go(9, right, self.split.A1, left)
        self.go(15, right, self.split.A, up)
        self.sib(up, self.split.B)
        self.sib(left, self.split.A)
        self.sib(right, self.split.A)
        self.got(1, left, self.split.B)
        self.go(4, left, self.split.B0, right)
        self.got(7, right, self.split.B)
        self.go(10, right, self.split.B1, left)
        self.sib(left, self.split.B)
        self.sib(right, self.split.B)

    def mid2(self):
        right, left, up = (1, 0), (-1, 0), (0, 1)
        self.got(2, (-1, 1), self.split.B)
        self.go(5, (-1, 1), self.split.B0, right)
        self.got(8, (1, 1), self.split.B)
        self.go(11, (1, 1), self.split.B1, left)
        self.sib((-1, 1), self.split.B)
        self.sib((1, 1), self.split.B)
        self.got(3, (2, 0), self.split.A0)
        self.got(9, (2, 0), self.split.A1)
        self.go(16, (2, 0), self.split.A, up)
        self.sib((2, 0), self.split.A)

    def fin(self):
        self.got(12, (0, 1), self.split.A)
        self.sib((0, 1), self.split.A)
        self.got(14, (-1, 1), self.split.A)
        self.sib((-1, 1), self.split.A)
        self.got(15, (1, 1), self.split.A)
        self.sib((1, 1), self.split.A)
        self.got(4, (2, 0), self.split.B0)
        self.got(10, (2, 0), self.split.B1)
        self.sib((2, 0), self.split.B)
        self.got(5, (2, 1), self.split.B0)
        self.got(11, (2, 1), self.split.B1)
        self.sib((2, 1), self.split.B)
        self.got(16, (2, 1), self.split.A)
        self.sib((2, 1), self.split.A)
        for i, where in enumerate(PLACES):
            for j, part in enumerate((self.split.A, self.split.B)):
                self.move.take(18 + 2 * i + j, self.buf.at[self.at.row(*where, part, 1)], self.at.peer(0, 0, 1))


class Scatter:
    ORDER = [2, 1, -1, 0]
    ROWS = 7 * SHARD + 8 * SHARD

    def __init__(self, place, split, buf, land, base, cols, send_sem, recv_sem):
        self.at, self.split, self.buf, self.land, self.cols = place, split, buf, land, cols
        self.move = Mover(send_sem, recv_sem)
        p = split
        parts = [p.B0, p.B0, p.A0, p.B, p.B, p.A, p.B1, p.B1, p.A1, p.B, p.B, p.A, p.A, p.A, p.A, p.A, p.B] + [p.whole] * 8
        self.sizes = [part[1] for part in parts]
        self.offsets = [base + sum(self.sizes[:i]) for i in range(len(parts))]

    def slot(self, key):
        return self.land.at[pl.ds(self.offsets[key], self.sizes[key]), self.cols]

    def go(self, key, where, part, to):
        if part[1]:
            rows = self.buf.at[self.at.row(*where, part), self.cols]
            self.move.send(key, rows, self.slot(key), self.at.peer(*to))

    def add(self, key, where, part):
        if part[1]:
            self.move.take(key, self.slot(key), self.at.peer(0, 1))
            rows = self.at.row(*where, part)
            total = self.buf[rows, self.cols].astype(F32) + self.slot(key)[...].astype(F32)
            self.buf[rows, self.cols] = total.astype(BF16)

    def block(self, dx):
        return pl.multiple_of(lax.rem(self.at.x + dx + 4, 4) * 256, 256)

    def share(self, dx):
        for dy in (1, 0):
            key = 17 + 2 * self.ORDER.index(dx) + dy
            rows = self.buf.at[self.at.row(dx, dy, self.split.whole, 1), self.cols]
            self.move.send(key, rows, self.slot(key), self.at.peer(0, 0, 1))

    def join(self, dx):
        right, left, up = (1, 0), (-1, 0), (0, 1)
        for dy in (1, 0):
            self.add(17 + 2 * self.ORDER.index(dx) + dy, (dx, dy), self.split.whole)
        if dx == 2:
            self.go(0, (2, 1), self.split.B0, left)
            self.go(6, (2, 1), self.split.B1, right)
            self.go(12, (2, 1), self.split.A, up)
            self.go(1, (2, 0), self.split.B0, left)
            self.go(7, (2, 0), self.split.B1, right)
        else:
            self.go({-1: 13, 1: 14, 0: 15}[dx], (dx, 1), self.split.A, up)

    def cross(self):
        right, left = (1, 0), (-1, 0)
        self.add(12, (2, 0), self.split.A)
        self.go(2, (2, 0), self.split.A0, left)
        self.go(8, (2, 0), self.split.A1, right)
        self.add(0, (-1, 1), self.split.B0)
        self.go(3, (-1, 1), self.split.B, left)
        self.add(6, (1, 1), self.split.B1)
        self.go(9, (1, 1), self.split.B, right)
        self.add(1, (-1, 0), self.split.B0)
        self.go(4, (-1, 0), self.split.B, left)
        self.add(7, (1, 0), self.split.B1)
        self.go(10, (1, 0), self.split.B, right)

    def cross2(self):
        right, left, up = (1, 0), (-1, 0), (0, 1)
        self.add(3, (0, 1), self.split.B)
        self.add(9, (0, 1), self.split.B)
        self.go(16, (0, 1), self.split.B, up)
        self.add(13, (-1, 0), self.split.A)
        self.add(2, (-1, 0), self.split.A0)
        self.go(5, (-1, 0), self.split.A, left)
        self.add(14, (1, 0), self.split.A)
        self.add(8, (1, 0), self.split.A1)
        self.go(11, (1, 0), self.split.A, right)

    def total(self, out, start=None):
        for part, keys in ((self.split.A, (15, 5, 11)), (self.split.B, (4, 10, 16))):
            rows = pl.ds(*part)
            whole = self.buf[self.at.row(0, 0, part), self.cols].astype(F32)
            for key in keys:
                self.move.take(key, self.slot(key), self.at.peer(0, 1))
                whole = whole + self.slot(key)[...].astype(F32)
            if start is not None:
                whole = whole + start[rows, self.cols].astype(F32)
            out[rows, self.cols] = whole.astype(out.dtype)


def softmax_block(q_blk, keys, first):
    rows, length = q_blk.shape[0], keys.shape[0]
    scale = 1.0 / math.sqrt(q_blk.shape[1])
    scores = dot(q_blk, keys, ((1,), (1,)))
    row_index = lax.broadcasted_iota(jnp.int32, (rows, length), 0) + first
    col_index = lax.broadcasted_iota(jnp.int32, (rows, length), 1)
    scores = jnp.where(col_index <= row_index, scores, NEG_FILL)
    weights = jnp.exp((scores - jnp.max(scores, axis=-1, keepdims=True)) * scale)
    return weights, jnp.sum(weights, axis=-1, keepdims=True)


def kernel(
    inc_hbm, parked, cot_hbm, gain, teacher, language, wq_hbm, wkv_hbm, wo_hbm,
    next_out, back_out, parkn_out, qg_out, kg_out, og_out, gain_out,
    g, land, wq, wkv, wo, og, inc, cot, stash, fwd_rows, back_rows, d_rows, q, kv, att, d_out, dq, dk, dv,
    dkv_send, dkv_recv, dkv, gain_send, gain_recv,
    ag_send, ag_recv, rs_send, rs_recv, misc_send, misc_recv, gs_send, gs_recv, local_sem,
):
    at = Place()
    length, width = g.shape[1], g.shape[2]
    blocks, ranks = length // 256, length // SHARD

    loads = [
        pltpu.make_async_copy(src, dst, local_sem.at[i])
        for i, (src, dst) in enumerate(
            ((inc_hbm, inc), (cot_hbm, cot), (wq_hbm, wq), (wkv_hbm, wkv), (wo_hbm, wo))
        )
    ]
    for load in loads:
        load.start()
    barrier = pltpu.get_barrier_semaphore()
    peers = [(at.s, lax.rem(at.d + k, ranks)) for k in range(1, ranks)] + [at.relay(4), at.relay(1), at.relay(-1)]
    for peer in peers:
        pl.semaphore_signal(barrier, inc=1, device_id=peer, device_id_type=MESH)

    own = at.row(0, 0, WHOLE)
    core = at.c

    def inverse_rms(values):
        return lax.rsqrt(jnp.mean(values * values, axis=-1, keepdims=True) + EPSILON)

    def normalized(rows):
        values = rows[...].astype(F32)
        return (values * inverse_rms(values) * gain[...]).astype(BF16)

    weight = jnp.exp2(-teacher[...].astype(F32)) * (0.5 + language[...].astype(F32) / (LANGS - 1))
    weight = jnp.where(at.s == lax.axis_size("section") - 1, weight, 1.0)
    square = lax.broadcasted_iota(jnp.int32, (SHARD, SHARD), 0) == lax.broadcasted_iota(jnp.int32, (SHARD, SHARD), 1)
    weight = jnp.sum(jnp.where(square, weight, 0.0), axis=1, keepdims=True)
    loads[0].wait()
    g[0, own, :] = normalized(inc)

    pl.semaphore_wait(barrier, len(peers))
    misc = Mover(misc_send, misc_recv)
    misc.send(0, parked, stash, at.relay(4))
    splits = (TILT_LEFT, EVEN, TILT_RIGHT)
    ag_f, ag_u, ag_b = [Gather(at, splits[i], g.at[i], ag_send.at[i], ag_recv.at[i]) for i in range(3)]
    ag_f.start()
    loads[1].wait()
    cot[...] = (cot[...].astype(F32) * weight).astype(BF16)
    g[1, own, :] = cot[...]
    ag_u.start()
    misc.send(1, inc, parkn_out, at.relay(4))
    ag_f.mid()
    misc.take(0, stash, at.relay(4))
    g[2, own, :] = normalized(stash)
    ag_b.start()
    ag_f.mid2()
    ag_u.mid()
    ag_f.fin()
    for load in loads[2:]:
        load.wait()

    def project(source, slot):
        def step(i, carry):
            rows = pl.ds(pl.multiple_of(i * 256, 256), 256)
            piece = g[source, rows, :]
            q[slot, rows, :] = dot(piece, wq[...]).astype(BF16)
            kv[slot, core, rows, :] = dot(piece, wkv[...]).astype(BF16)
            return carry

        lax.fori_loop(0, blocks, step, 0)
        misc.send(2 + slot, kv.at[slot, core], kv.at[slot, core], at.peer(0, 0, 1))

    def keyval_arrived(slot):
        misc.take(2 + slot, kv.at[slot, 1 - core], at.peer(0, 0, 1))

    def attend(head):
        cols = pl.ds(head * 128, 128)
        for i in range(blocks):
            rows, seen = pl.ds(i * 256, 256), pl.ds(0, (i + 1) * 256)
            weights, norm = softmax_block(q[0, rows, cols], kv[0, 0, seen, :], i * 256)
            att[0, rows, cols] = (dot(weights.astype(BF16), kv[0, 1, seen, :]) / norm).astype(BF16)

    def attend_back(head):
        cols = pl.ds(head * 128, 128)
        for i in range(blocks):
            rows, seen = pl.ds(i * 256, 256), pl.ds(0, (i + 1) * 256)
            q_blk, keys, vals = q[1, rows, cols], kv[1, 0, seen, :], kv[1, 1, seen, :]
            weights, norm = softmax_block(q_blk, keys, i * 256)
            weights = weights / norm
            rounded = weights.astype(BF16)
            att[1, rows, cols] = dot(rounded, vals).astype(BF16)
            d_blk = d_out[rows, cols]
            d_weights = dot(d_blk, vals, ((1,), (1,)))
            delta = jnp.sum(weights * d_weights, axis=-1, keepdims=True)
            d_scores = (weights * (d_weights - delta) * scale).astype(BF16)
            dq[rows, cols] = dot(d_scores, keys).astype(BF16)
            dk[seen, :] += dot(d_scores, q_blk, ((0,), (0,)))
            dv[seen, :] += dot(rounded, d_blk, ((0,), (0,)))

    half = width // 2
    halves = [pl.ds(0, half), pl.ds(half, half)]
    rows_of = Scatter.ROWS // 2
    rs_f = [
        Scatter(at, split, g.at[0], land.at[0], 0, halves[h], rs_send.at[h], rs_recv.at[h])
        for h, split in enumerate((TILT_RIGHT, TILT_LEFT))
    ]
    rs_b = [
        Scatter(at, split, g.at[1], land.at[1], h * rows_of, pl.ds(0, width), rs_send.at[2 + h], rs_recv.at[2 + h])
        for h, split in enumerate((UPPER, LOWER))
    ]

    def produce(dx, buf, first, count, term):
        rows = pl.ds(rs_f[0].block(dx), 256)

        def step(j, carry):
            cols = pl.ds(pl.multiple_of(first + j * 1024, 1024), 1024)
            g[buf, rows, cols] = term(rows, cols).astype(BF16)
            return carry

        lax.fori_loop(0, count // 1024, step, 0)

    def forward_term(rows, cols):
        return dot(att[0, rows, :], wo[:, cols])

    def back_term(rows, cols):
        term = dot(dq[rows, :], wq[cols, :], ((1,), (1,)))
        return term + dot(dkv[rows, :], wkv[cols, :], ((1,), (1,)))

    project(0, 0)
    ag_u.mid2()
    ag_b.mid()
    keyval_arrived(0)
    attend(0)
    ag_u.fin()
    attend(1)
    ag_b.mid2()
    ag_f.move.drain()
    for h, sums in enumerate(rs_f):
        for i, dx in enumerate(Scatter.ORDER):
            produce(dx, 0, h * half, half, forward_term)
            sums.share(dx)
            if i:
                sums.join(Scatter.ORDER[i - 1])
        sums.join(0)

    def cotangent_step(i, carry):
        rows = pl.ds(pl.multiple_of(i * 256, 256), 256)
        d_out[rows, :] = dot(g[1, rows, :], wo[...], ((1,), (1,))).astype(BF16)
        return carry

    lax.fori_loop(0, blocks, cotangent_step, 0)
    ag_b.fin()
    project(2, 1)
    dk[...] = jnp.zeros_like(dk)
    dv[...] = jnp.zeros_like(dv)
    scale = 1.0 / math.sqrt(dk.shape[1])
    rs_f[0].cross()
    keyval_arrived(1)
    attend_back(0)
    rs_f[1].cross()
    attend_back(1)
    even = core == 0
    dkv_send[...] = jnp.where(even, dv[...], dk[...]).astype(BF16)
    misc.send(4, dkv_send, dkv_recv, at.peer(0, 0, 1))
    att_t = att[1].T

    def output_grad_step(j, carry):
        cols = pl.ds(pl.multiple_of(j * 512, 512), 512)
        og[:, cols] = dot(att_t, g[1, :, cols]).astype(BF16)
        return carry

    lax.fori_loop(0, width // 512, output_grad_step, 0)
    og_copy = pltpu.make_async_copy(og, og_out, local_sem.at[5])
    og_copy.start()
    rs_f[0].cross2()
    misc.take(4, dkv_recv, at.peer(0, 0, 1))
    dkv[...] = (jnp.where(even, dk[...], dv[...]) + dkv_recv[...].astype(F32)).astype(BF16)
    ag_u.move.drain()

    for i, dx in enumerate(Scatter.ORDER):
        produce(dx, 1, 0, width, back_term)
        for sums in rs_b:
            sums.share(dx)
        if i:
            for sums in rs_b:
                sums.join(Scatter.ORDER[i - 1])
    for sums in rs_b:
        sums.join(0)
    rs_f[1].cross2()
    rs_b[0].cross()

    for h, sums in enumerate(rs_f):
        sums.total(fwd_rows, inc)
        misc.send(7 + h, fwd_rows.at[:, halves[h]], next_out.at[:, halves[h]], at.relay(1))
    rs_b[1].cross()

    grad_t = jnp.concatenate([dq[...], dkv[...]], axis=1).T

    def weight_grad_step(j, carry):
        cols = pl.ds(pl.multiple_of(j * 512, 512), 512)
        block = dot(grad_t, g[2, :, cols]).astype(BF16).T
        wq[cols, :] = block[:, :256]
        wkv[cols, :] = block[:, 256:]
        return carry

    steps = width // 512
    lax.fori_loop(0, steps // 2, weight_grad_step, 0)
    rs_b[0].cross2()
    lax.fori_loop(steps // 2, steps, weight_grad_step, 0)
    qg_copy = pltpu.make_async_copy(wq, qg_out, local_sem.at[6])
    kg_copy = pltpu.make_async_copy(wkv, kg_out, local_sem.at[7])
    qg_copy.start()
    kg_copy.start()
    rs_b[1].cross2()

    d_gain = jnp.zeros((1, width), F32)
    for i, sums in enumerate(rs_b):
        sums.total(d_rows)
        rows = pl.ds(i * 32, 32)
        d_normed = d_rows[rows, :]
        values = stash[rows, :].astype(F32)
        inverse = inverse_rms(values)
        scaled = d_normed * gain[...]
        inner = jnp.mean(scaled * values, axis=-1, keepdims=True)
        change = inverse * scaled - values * (inverse * inverse * inverse * inner)
        back_rows[rows, :] = (cot[rows, :].astype(F32) + change).astype(BF16)
        misc.send(5 + i, back_rows.at[rows], back_out.at[rows], at.relay(-1))
        d_gain = d_gain + jnp.sum(d_normed * (values * inverse), axis=0, keepdims=True)
    gains = Mover(gs_send, gs_recv)
    piece = width // ranks
    for k in range(ranks):
        gain_send[k] = d_gain[:, k * piece:(k + 1) * piece]
    for k in range(1, ranks):
        there = lax.rem(at.d + k, ranks)
        gains.send(k, gain_send.at[there], gain_recv.at[k], (at.s, there))
    gain_sum = gain_send[at.d]
    for k in range(1, ranks):
        gains.take(k, gain_recv.at[k], (at.s, lax.rem(at.d + k, ranks)))
        gain_sum = gain_sum + gain_recv[k]
    gain_out[...] = gain_sum

    for copy in (og_copy, qg_copy, kg_copy):
        copy.wait()
    for mover in [ag_b.move, gains] + [sums.move for sums in rs_f + rs_b]:
        mover.drain()
    misc.take(1, parkn_out, at.relay(4))
    for i in range(2):
        misc.take(5 + i, back_out.at[pl.ds(i * 32, 32)], at.relay(1))
        misc.take(7 + i, next_out.at[:, halves[i]], at.relay(-1))
    misc.drain()


def deliver(*refs):
    count = (len(refs) - 1) // 3
    sem, held = refs[-1], refs[2 * count:3 * count]
    into = [pltpu.make_async_copy(refs[i], held[i], sem.at[i]) for i in range(count)]
    out = [pltpu.make_async_copy(held[i], refs[count + i], sem.at[count + i]) for i in range(count)]
    for copy in into:
        copy.start()
    for first, second in zip(into, out):
        first.wait()
        second.start()
    for copy in out:
        copy.wait()


def cycle(inc, parked, cot, gain, teacher, language, wq, wkv, wo):
    tokens, width = inc.shape
    ranks = lax.axis_size("dp")
    length = tokens * ranks
    any_spec = pl.BlockSpec(memory_space=pl.ANY)
    vmem_spec = pl.BlockSpec(memory_space=pltpu.VMEM)
    block = jax.ShapeDtypeStruct((tokens, width), BF16)
    shapes = [block, block, block] + [jax.ShapeDtypeStruct(w.shape, BF16) for w in (wq, wkv, wo)]
    heads_width, head_dim = wq.shape[1], wkv.shape[1]
    scratch = [
        pltpu.VMEM((3, length, width), BF16),
        pltpu.VMEM((2, Scatter.ROWS, width), BF16),
        pltpu.VMEM(wq.shape, BF16),
        pltpu.VMEM(wkv.shape, BF16),
        pltpu.VMEM(wo.shape, BF16),
        pltpu.VMEM(wo.shape, BF16),
        pltpu.VMEM((tokens, width), BF16),
        pltpu.VMEM((tokens, width), BF16),
        pltpu.VMEM((tokens, width), BF16),
        pltpu.VMEM((tokens, width), BF16),
        pltpu.VMEM((tokens, width), BF16),
        pltpu.VMEM((tokens, width), F32),
        pltpu.VMEM((2, length, heads_width), BF16),
        pltpu.VMEM((2, 2, length, head_dim), BF16),
        pltpu.VMEM((2, length, heads_width), BF16),
        pltpu.VMEM((length, heads_width), BF16),
        pltpu.VMEM((length, heads_width), BF16),
        pltpu.VMEM((length, head_dim), F32),
        pltpu.VMEM((length, head_dim), F32),
        pltpu.VMEM((length, head_dim), BF16),
        pltpu.VMEM((length, head_dim), BF16),
        pltpu.VMEM((length, head_dim), BF16),
        pltpu.VMEM((ranks, 1, width // ranks), F32),
        pltpu.VMEM((ranks, 1, width // ranks), F32),
        pltpu.SemaphoreType.DMA((3, 34)),
        pltpu.SemaphoreType.DMA((3, 34)),
        pltpu.SemaphoreType.DMA((4, 25)),
        pltpu.SemaphoreType.DMA((4, 25)),
        pltpu.SemaphoreType.DMA((9,)),
        pltpu.SemaphoreType.DMA((9,)),
        pltpu.SemaphoreType.DMA((ranks,)),
        pltpu.SemaphoreType.DMA((ranks,)),
        pltpu.SemaphoreType.DMA((8,)),
    ]
    results = pl.pallas_call(
        kernel,
        out_shape=shapes + [jax.ShapeDtypeStruct((1, width // ranks), F32)],
        in_specs=[any_spec, any_spec, any_spec, vmem_spec, vmem_spec, vmem_spec, any_spec, any_spec, any_spec],
        out_specs=[any_spec] * 6 + [vmem_spec],
        scratch_shapes=scratch,
        compiler_params=pltpu.CompilerParams(
            collective_id=0, has_side_effects=True, vmem_limit_bytes=62 * 2**20
        ),
        cost_estimate=pl.CostEstimate(flops=24 * 10**9, bytes_accessed=2 * 10**7, transcendentals=4 * 10**6),
        name="relay_cycle",
    )(inc, parked, cot, gain, teacher, language, wq, wkv, wo)
    delivered = pl.pallas_call(
        deliver,
        out_shape=shapes,
        in_specs=[any_spec] * 6,
        out_specs=[any_spec] * 6,
        scratch_shapes=[pltpu.VMEM(shape.shape, BF16) for shape in shapes] + [pltpu.SemaphoreType.DMA((12,))],
        compiler_params=pltpu.CompilerParams(vmem_limit_bytes=62 * 2**20),
        name="deliver",
    )(*results[:6])
    return (*delivered, results[6])


def body(
    incoming,
    parked,
    cotangent,
    norm_gain,
    query_weight,
    keyval_weight,
    output_weight,
    teacher_id,
    language_id,
):
    results = cycle(
        incoming[0], parked[0], cotangent[0], norm_gain, teacher_id[None], language_id[None],
        query_weight[0], keyval_weight[0], output_weight[0],
    )
    return tuple(item[None] for item in results[:6]) + (results[6],)


def solution(mesh):
    return jax.shard_map(
        body,
        mesh=mesh,
        in_specs=(
            P("section", "dp", None),
            P("section", "dp", None),
            P("section", "dp", None),
            P("section", None),
            P("section", None, "dp"),
            P("section", None, "dp"),
            P("section", "dp", None),
            P("dp"),
            P("dp"),
        ),
        out_specs=(
            P("section", "dp", None),
            P("section", "dp", None),
            P("section", "dp", None),
            P("section", None, "dp"),
            P("section", None, "dp"),
            P("section", "dp", None),
            P("section", "dp"),
        ),
        check_vma=False,
    )
```

```python
import functools
import math

import jax
import jax.numpy as jnp
from jax import lax
from jax.experimental import pallas as pl
from jax.experimental.pallas import tpu as pltpu
from jax.sharding import PartitionSpec as P

LANGS = 16
EPSILON = 1e-05
NEG_FILL = -1e30
MESH = pl.DeviceIdType.MESH
BF16 = jnp.bfloat16
F32 = jnp.float32

SHARD = 64
WHOLE = (0, 64)
PLACES = [(0, 0), (0, 1), (-1, 0), (1, 0), (2, 0), (-1, 1), (1, 1), (2, 1)]


def dot(a, b, dims=((1,), (0,))):
    return lax.dot_general(a, b, (dims, ((), ())), preferred_element_type=F32)


class Split:
    def __init__(self, low, a_cut, middle, b_cut, high):
        self.whole = (low, high - low)
        self.A, self.A0, self.A1 = (low, middle - low), (low, a_cut - low), (a_cut, middle - a_cut)
        self.B, self.B0, self.B1 = (middle, high - middle), (middle, b_cut - middle), (b_cut, high - b_cut)


EVEN = Split(0, 16, 32, 48, 64)
TILT_RIGHT = Split(0, 16, 16, 32, 64)
TILT_LEFT = Split(0, 0, 16, 48, 64)
UPPER = Split(0, 16, 16, 16, 32)
LOWER = Split(32, 32, 48, 64, 64)


SEQUENCE = [
    "fs", "fm1", "fm2", "bs", "ffin1", "fm3", "fn1", "fn2", "us", "bm1", "ffin2", "ffin3", "um1", "bm3",
    "bm2", "projf", "att0", "att1", "pf00", "bfin1", "bn1", "um2", "rf0j0", "pf02", "un1", "pf01", "pf10",
    "um3", "rf0j2", "pf1-1", "pf11", "bn2", "pf0-1", "ufin1", "rf1j0", "pf12", "bfin2", "un2", "rf0j-1",
    "bfin3", "projb", "rf1j1", "rf0j1", "ufin2", "rf1j2", "rf0B", "rf1j-1", "ufin3", "cot", "rf1B", "rf0A",
    "back0", "rf0D", "rf0C", "back1", "rf0E", "dkv", "rf1D", "og", "rf0T", "dkvt", "pb2", "pb-1", "rf1C",
    "rb0j2", "pb1", "rb0j-1", "rf1A", "pb0", "rb0j1", "rb0B", "rb0j0", "rb1j0", "rb0A", "g1", "rb1j2", "rb0C",
    "rb1j-1", "rb1A", "rb1j1", "rb1B", "rf1E", "g0", "rb0D", "rb0E", "rb1D", "g3", "rb1E", "rf1T", "rb0T",
    "g2", "rb1C", "rb1T",
]
GATHER_SPLITS = (EVEN, EVEN, TILT_LEFT)
SCATTER_SPLITS = (TILT_LEFT, EVEN)


class Place:
    def __init__(self):
        self.s = lax.axis_index("section")
        self.d = lax.axis_index("dp")
        self.x = self.d // 4
        self.y = lax.rem(self.d // 2, 2)
        self.c = lax.rem(self.d, 2)

    def index(self, dx, dy, flip=0):
        x = lax.rem(self.x + dx + 4, 4)
        y = self.y if dy == 0 else 1 - self.y
        c = self.c if flip == 0 else 1 - self.c
        return x * 4 + y * 2 + c

    def row(self, dx, dy, part, flip=0):
        start = self.index(dx, dy, flip) * SHARD + part[0]
        return pl.ds(pl.multiple_of(start, 16), part[1])

    def peer(self, dx, dy, flip=0):
        return (self.s, self.index(dx, dy, flip))

    def relay(self, steps):
        return (lax.rem(self.s + steps + 8, 8), self.d)


class Mover:
    def __init__(self, send_sem, recv_sem):
        self.send_sem, self.recv_sem = send_sem, recv_sem
        self.open = []

    def send(self, key, src, dst, target):
        copy = pltpu.make_async_remote_copy(
            src_ref=src, dst_ref=dst, send_sem=self.send_sem.at[key], recv_sem=self.recv_sem.at[key],
            device_id=target, device_id_type=MESH,
        )
        copy.start()
        self.open.append(copy)

    def take(self, key, dst, source):
        pltpu.make_async_remote_copy(
            src_ref=dst, dst_ref=dst, send_sem=self.send_sem.at[key], recv_sem=self.recv_sem.at[key],
            device_id=source, device_id_type=MESH,
        ).wait_recv()

    def drain(self):
        for copy in self.open:
            copy.wait_send()
        self.open = []


class Gather:
    def __init__(self, place, split, buf, send_sem, recv_sem):
        self.at, self.split, self.buf = place, split, buf
        self.move = Mover(send_sem, recv_sem)

    def go(self, key, where, part, to):
        if part[1]:
            rows = self.buf.at[self.at.row(*where, part)]
            self.move.send(key, rows, rows, self.at.peer(*to))

    def sib(self, where, part):
        key = 18 + 2 * PLACES.index(where) + (0 if part == self.split.A else 1)
        rows = self.buf.at[self.at.row(*where, part)]
        self.move.send(key, rows, rows, self.at.peer(0, 0, 1))

    def got(self, key, where, part):
        if part[1]:
            self.move.take(key, self.buf.at[self.at.row(*where, part)], self.at.peer(0, 1))

    def start(self):
        own, right, left, up = (0, 0), (1, 0), (-1, 0), (0, 1)
        self.go(13, own, self.split.B, up)
        self.go(0, own, self.split.A, right)
        self.go(6, own, self.split.A, left)
        self.go(12, own, self.split.A, up)
        self.go(1, own, self.split.B, right)
        self.go(7, own, self.split.B, left)
        self.sib(own, self.split.A)
        self.sib(own, self.split.B)

    def m1(self):
        self.got(13, (0, 1), self.split.B)
        self.go(2, (0, 1), self.split.B, (1, 0))
        self.go(8, (0, 1), self.split.B, (-1, 0))
        self.sib((0, 1), self.split.B)

    def m2(self):
        self.got(0, (-1, 0), self.split.A)
        self.go(3, (-1, 0), self.split.A0, (1, 0))
        self.go(14, (-1, 0), self.split.A, (0, 1))
        self.got(6, (1, 0), self.split.A)
        self.go(9, (1, 0), self.split.A1, (-1, 0))
        self.go(15, (1, 0), self.split.A, (0, 1))
        self.sib((-1, 0), self.split.A)
        self.sib((1, 0), self.split.A)

    def m3(self):
        self.got(1, (-1, 0), self.split.B)
        self.go(4, (-1, 0), self.split.B0, (1, 0))
        self.got(7, (1, 0), self.split.B)
        self.go(10, (1, 0), self.split.B1, (-1, 0))
        self.sib((-1, 0), self.split.B)
        self.sib((1, 0), self.split.B)

    def n1(self):
        self.got(2, (-1, 1), self.split.B)
        self.go(5, (-1, 1), self.split.B0, (1, 0))
        self.got(8, (1, 1), self.split.B)
        self.go(11, (1, 1), self.split.B1, (-1, 0))
        self.sib((-1, 1), self.split.B)
        self.sib((1, 1), self.split.B)

    def n2(self):
        self.got(3, (2, 0), self.split.A0)
        self.got(9, (2, 0), self.split.A1)
        self.go(16, (2, 0), self.split.A, (0, 1))
        self.sib((2, 0), self.split.A)

    def fin1(self):
        for key, where in ((12, (0, 1)), (14, (-1, 1)), (15, (1, 1))):
            self.got(key, where, self.split.A)
            self.sib(where, self.split.A)

    def fin2(self):
        self.got(4, (2, 0), self.split.B0)
        self.got(10, (2, 0), self.split.B1)
        self.sib((2, 0), self.split.B)
        self.got(5, (2, 1), self.split.B0)
        self.got(11, (2, 1), self.split.B1)
        self.sib((2, 1), self.split.B)
        self.got(16, (2, 1), self.split.A)
        self.sib((2, 1), self.split.A)

    def fin3(self):
        for i, where in enumerate(PLACES):
            for j, part in enumerate((self.split.A, self.split.B)):
                self.move.take(18 + 2 * i + j, self.buf.at[self.at.row(*where, part, 1)], self.at.peer(0, 0, 1))


class Scatter:
    ORDER = [2, 1, -1, 0]
    ROWS = 7 * SHARD + 8 * SHARD

    def __init__(self, place, split, buf, land, base, cols, send_sem, recv_sem):
        self.at, self.split, self.buf, self.land, self.cols = place, split, buf, land, cols
        self.move = Mover(send_sem, recv_sem)
        p = split
        parts = [p.B0, p.B0, p.A0, p.B, p.B, p.A, p.B1, p.B1, p.A1, p.B, p.B, p.A, p.A, p.A, p.A, p.A, p.B] + [p.whole] * 8
        self.sizes = [part[1] for part in parts]
        self.offsets = [base + sum(self.sizes[:i]) for i in range(len(parts))]

    def slot(self, key):
        return self.land.at[pl.ds(self.offsets[key], self.sizes[key]), self.cols]

    def go(self, key, where, part, to):
        if part[1]:
            rows = self.buf.at[self.at.row(*where, part), self.cols]
            self.move.send(key, rows, self.slot(key), self.at.peer(*to))

    def add(self, key, where, part):
        if part[1]:
            self.move.take(key, self.slot(key), self.at.peer(0, 1))
            rows = self.at.row(*where, part)
            total = self.buf[rows, self.cols].astype(F32) + self.slot(key)[...].astype(F32)
            self.buf[rows, self.cols] = total.astype(BF16)

    def block(self, dx):
        return pl.multiple_of(lax.rem(self.at.x + dx + 4, 4) * 256, 256)

    def share(self, dx):
        for dy in (1, 0):
            key = 17 + 2 * self.ORDER.index(dx) + dy
            rows = self.buf.at[self.at.row(dx, dy, self.split.whole, 1), self.cols]
            self.move.send(key, rows, self.slot(key), self.at.peer(0, 0, 1))

    def join(self, dx):
        right, left, up = (1, 0), (-1, 0), (0, 1)
        for dy in (1, 0):
            self.add(17 + 2 * self.ORDER.index(dx) + dy, (dx, dy), self.split.whole)
        if dx == 2:
            self.go(0, (2, 1), self.split.B0, left)
            self.go(6, (2, 1), self.split.B1, right)
            self.go(12, (2, 1), self.split.A, up)
            self.go(1, (2, 0), self.split.B0, left)
            self.go(7, (2, 0), self.split.B1, right)
        else:
            self.go({-1: 13, 1: 14, 0: 15}[dx], (dx, 1), self.split.A, up)

    def cross_a(self):
        self.add(12, (2, 0), self.split.A)
        self.go(2, (2, 0), self.split.A0, (-1, 0))
        self.go(8, (2, 0), self.split.A1, (1, 0))

    def cross_b(self):
        self.add(0, (-1, 1), self.split.B0)
        self.go(3, (-1, 1), self.split.B, (-1, 0))
        self.add(6, (1, 1), self.split.B1)
        self.go(9, (1, 1), self.split.B, (1, 0))

    def cross_c(self):
        self.add(1, (-1, 0), self.split.B0)
        self.go(4, (-1, 0), self.split.B, (-1, 0))
        self.add(7, (1, 0), self.split.B1)
        self.go(10, (1, 0), self.split.B, (1, 0))

    def cross_d(self):
        self.add(3, (0, 1), self.split.B)
        self.add(9, (0, 1), self.split.B)
        self.go(16, (0, 1), self.split.B, (0, 1))

    def cross_e(self):
        self.add(13, (-1, 0), self.split.A)
        self.add(2, (-1, 0), self.split.A0)
        self.go(5, (-1, 0), self.split.A, (-1, 0))
        self.add(14, (1, 0), self.split.A)
        self.add(8, (1, 0), self.split.A1)
        self.go(11, (1, 0), self.split.A, (1, 0))

    def total(self, out, start=None):
        for part, keys in ((self.split.A, (15, 5, 11)), (self.split.B, (4, 10, 16))):
            rows = pl.ds(*part)
            whole = self.buf[self.at.row(0, 0, part), self.cols].astype(F32)
            for key in keys:
                self.move.take(key, self.slot(key), self.at.peer(0, 1))
                whole = whole + self.slot(key)[...].astype(F32)
            if start is not None:
                whole = whole + start[rows, self.cols].astype(F32)
            out[rows, self.cols] = whole.astype(out.dtype)


def softmax_block(q_blk, keys, first):
    rows, length = q_blk.shape[0], keys.shape[0]
    scale = 1.0 / math.sqrt(q_blk.shape[1])
    scores = dot(q_blk, keys, ((1,), (1,)))
    row_index = lax.broadcasted_iota(jnp.int32, (rows, length), 0) + first
    col_index = lax.broadcasted_iota(jnp.int32, (rows, length), 1)
    scores = jnp.where(col_index <= row_index, scores, NEG_FILL)
    weights = jnp.exp((scores - jnp.max(scores, axis=-1, keepdims=True)) * scale)
    return weights, jnp.sum(weights, axis=-1, keepdims=True)


def kernel(
    inc_hbm, parked, cot_hbm, gain, teacher, language, wq_hbm, wkv_hbm, wo_hbm,
    next_out, back_out, parkn_out, qg_out, kg_out, og_out, gain_out,
    g, land, wq, wkv, wo, og, inc, cot, stash, fwd_rows, back_rows, d_rows, q, kv, att, d_out, dq, dk, dv,
    dkv_send, dkv_recv, dkv, gain_send, gain_recv,
    ag_send, ag_recv, rs_send, rs_recv, misc_send, misc_recv, gs_send, gs_recv, local_sem,
):
    at = Place()
    length, width = g.shape[1], g.shape[2]
    blocks, ranks = length // 256, length // SHARD

    loads = [
        pltpu.make_async_copy(src, dst, local_sem.at[i])
        for i, (src, dst) in enumerate(
            ((inc_hbm, inc), (cot_hbm, cot), (wq_hbm, wq), (wkv_hbm, wkv), (wo_hbm, wo))
        )
    ]
    for load in loads:
        load.start()
    barrier = pltpu.get_barrier_semaphore()
    peers = [(at.s, lax.rem(at.d + k, ranks)) for k in range(1, ranks)] + [at.relay(4), at.relay(1), at.relay(-1)]
    for peer in peers:
        pl.semaphore_signal(barrier, inc=1, device_id=peer, device_id_type=MESH)

    own = at.row(0, 0, WHOLE)
    core = at.c

    def inverse_rms(values):
        return lax.rsqrt(jnp.mean(values * values, axis=-1, keepdims=True) + EPSILON)

    def normalized(rows):
        values = rows[...].astype(F32)
        return (values * inverse_rms(values) * gain[...]).astype(BF16)

    weight = jnp.exp2(-teacher[...].astype(F32)) * (0.5 + language[...].astype(F32) / (LANGS - 1))
    weight = jnp.where(at.s == lax.axis_size("section") - 1, weight, 1.0)
    square = lax.broadcasted_iota(jnp.int32, (SHARD, SHARD), 0) == lax.broadcasted_iota(jnp.int32, (SHARD, SHARD), 1)
    weight = jnp.sum(jnp.where(square, weight, 0.0), axis=1, keepdims=True)
    loads[0].wait()
    g[0, own, :] = normalized(inc)

    pl.semaphore_wait(barrier, len(peers))
    misc = Mover(misc_send, misc_recv)
    misc.send(0, parked, stash, at.relay(4))
    ag = {
        name: Gather(at, split, g.at[i], ag_send.at[i], ag_recv.at[i])
        for i, (name, split) in enumerate(zip("fub", GATHER_SPLITS))
    }
    loaded = set()

    def loads_done(*names):
        for name in names:
            if name not in loaded:
                loaded.add(name)
                loads[name].wait()

    def start_u():
        loads_done(1)
        cot[...] = (cot[...].astype(F32) * weight).astype(BF16)
        g[1, own, :] = cot[...]
        ag["u"].start()

    def start_b():
        misc.take(0, stash, at.relay(4))
        g[2, own, :] = normalized(stash)
        ag["b"].start()

    def project(source, slot):
        loads_done(2, 3)

        def step(i, carry):
            rows = pl.ds(pl.multiple_of(i * 256, 256), 256)
            piece = g[source, rows, :]
            q[slot, rows, :] = dot(piece, wq[...]).astype(BF16)
            kv[slot, core, rows, :] = dot(piece, wkv[...]).astype(BF16)
            return carry

        lax.fori_loop(0, blocks, step, 0)
        misc.send(2 + slot, kv.at[slot, core], kv.at[slot, core], at.peer(0, 0, 1))

    def keyval_arrived(slot):
        misc.take(2 + slot, kv.at[slot, 1 - core], at.peer(0, 0, 1))

    def attend(head):
        cols = pl.ds(head * 128, 128)
        for i in range(blocks):
            rows, seen = pl.ds(i * 256, 256), pl.ds(0, (i + 1) * 256)
            weights, norm = softmax_block(q[0, rows, cols], kv[0, 0, seen, :], i * 256)
            att[0, rows, cols] = (dot(weights.astype(BF16), kv[0, 1, seen, :]) / norm).astype(BF16)

    def attend_back(head):
        cols = pl.ds(head * 128, 128)
        for i in range(blocks):
            rows, seen = pl.ds(i * 256, 256), pl.ds(0, (i + 1) * 256)
            q_blk, keys, vals = q[1, rows, cols], kv[1, 0, seen, :], kv[1, 1, seen, :]
            weights, norm = softmax_block(q_blk, keys, i * 256)
            weights = weights / norm
            rounded = weights.astype(BF16)
            att[1, rows, cols] = dot(rounded, vals).astype(BF16)
            d_blk = d_out[rows, cols]
            d_weights = dot(d_blk, vals, ((1,), (1,)))
            delta = jnp.sum(weights * d_weights, axis=-1, keepdims=True)
            d_scores = (weights * (d_weights - delta) * scale).astype(BF16)
            dq[rows, cols] = dot(d_scores, keys).astype(BF16)
            dk[seen, :] += dot(d_scores, q_blk, ((0,), (0,)))
            dv[seen, :] += dot(rounded, d_blk, ((0,), (0,)))

    half = width // 2
    halves = [pl.ds(0, half), pl.ds(half, half)]
    rows_of = Scatter.ROWS // 2
    rs_f = [
        Scatter(at, split, g.at[0], land.at[0], 0, halves[h], rs_send.at[h], rs_recv.at[h])
        for h, split in enumerate(SCATTER_SPLITS)
    ]
    rs_b = [
        Scatter(at, split, g.at[1], land.at[1], h * rows_of, pl.ds(0, width), rs_send.at[2 + h], rs_recv.at[2 + h])
        for h, split in enumerate((UPPER, LOWER))
    ]

    def produce(dx, buf, first, count, term):
        rows = pl.ds(rs_f[0].block(dx), 256)

        def step(j, carry):
            cols = pl.ds(pl.multiple_of(first + j * 1024, 1024), 1024)
            g[buf, rows, cols] = term(rows, cols).astype(BF16)
            return carry

        lax.fori_loop(0, count // 1024, step, 0)

    def forward_term(rows, cols):
        return dot(att[0, rows, :], wo[:, cols])

    def back_term(rows, cols):
        term = dot(dq[rows, :], wq[cols, :], ((1,), (1,)))
        return term + dot(dkv[rows, :], wkv[cols, :], ((1,), (1,)))

    def cotangent():
        loads_done(4)

        def step(i, carry):
            rows = pl.ds(pl.multiple_of(i * 256, 256), 256)
            d_out[rows, :] = dot(g[1, rows, :], wo[...], ((1,), (1,))).astype(BF16)
            return carry

        lax.fori_loop(0, blocks, step, 0)

    arrived = set()

    def once(key, act):
        if key not in arrived:
            arrived.add(key)
            act()

    def attend_forward(head):
        once("keyval f", lambda: keyval_arrived(0))
        attend(head)

    def attend_backward(head):
        if head == 0:
            dk[...] = jnp.zeros_like(dk)
            dv[...] = jnp.zeros_like(dv)
            keyval_arrived(1)
        attend_back(head)

    scale = 1.0 / math.sqrt(dk.shape[1])
    even = core == 0

    def swap_keyval():
        dkv_send[...] = jnp.where(even, dv[...], dk[...]).astype(BF16)
        misc.send(4, dkv_send, dkv_recv, at.peer(0, 0, 1))

    def take_keyval():
        misc.take(4, dkv_recv, at.peer(0, 0, 1))
        dkv[...] = (jnp.where(even, dk[...], dv[...]) + dkv_recv[...].astype(F32)).astype(BF16)

    def output_grad():
        att_t = att[1].T

        def step(j, carry):
            cols = pl.ds(pl.multiple_of(j * 512, 512), 512)
            og[:, cols] = dot(att_t, g[1, :, cols]).astype(BF16)
            return carry

        lax.fori_loop(0, width // 512, step, 0)
        copies[0].start()

    def forward_block(h, dx):
        once("drain f", ag["f"].move.drain)
        loads_done(4)
        produce(dx, 0, h * half, half, forward_term)
        rs_f[h].share(dx)

    def back_block(dx):
        once("drain u", ag["u"].move.drain)
        produce(dx, 1, 0, width, back_term)
        for sums in rs_b:
            sums.share(dx)

    def weight_grads(quarter):
        grad_t = jnp.concatenate([dq[...], dkv[...]], axis=1).T

        def step(j, carry):
            cols = pl.ds(pl.multiple_of(j * 512, 512), 512)
            block = dot(grad_t, g[2, :, cols]).astype(BF16).T
            wq[cols, :] = block[:, :256]
            wkv[cols, :] = block[:, 256:]
            return carry

        steps = width // 2048
        lax.fori_loop(quarter * steps, (quarter + 1) * steps, step, 0)

    def finish_forward(h):
        rs_f[h].total(fwd_rows, inc)
        misc.send(7 + h, fwd_rows.at[:, halves[h]], next_out.at[:, halves[h]], at.relay(1))

    gain_parts = []

    def finish_back(h):
        rs_b[h].total(d_rows)
        rows = pl.ds(h * 32, 32)
        d_normed = d_rows[rows, :]
        values = stash[rows, :].astype(F32)
        inverse = inverse_rms(values)
        scaled = d_normed * gain[...]
        inner = jnp.mean(scaled * values, axis=-1, keepdims=True)
        change = inverse * scaled - values * (inverse * inverse * inverse * inner)
        back_rows[rows, :] = (cot[rows, :].astype(F32) + change).astype(BF16)
        misc.send(5 + h, back_rows.at[rows], back_out.at[rows], at.relay(-1))
        gain_parts.append(jnp.sum(d_normed * (values * inverse), axis=0, keepdims=True))
        if len(gain_parts) == 2:
            d_gain = gain_parts[0] + gain_parts[1]
            for k in range(ranks):
                gain_send[k] = d_gain[:, k * piece:(k + 1) * piece]
            for k in range(1, ranks):
                there = lax.rem(at.d + k, ranks)
                gains.send(k, gain_send.at[there], gain_recv.at[k], (at.s, there))

    gains = Mover(gs_send, gs_recv)
    piece = width // ranks
    copies = [
        pltpu.make_async_copy(src, dst, local_sem.at[5 + i])
        for i, (src, dst) in enumerate(((og, og_out), (wq, qg_out), (wkv, kg_out)))
    ]

    steps = {
        "fs": ag["f"].start, "us": start_u, "bs": start_b,
        "projf": lambda: project(0, 0), "projb": lambda: project(2, 1), "cot": cotangent,
        "dkv": swap_keyval, "dkvt": take_keyval, "og": output_grad,
    }
    for name, gather in ag.items():
        for stage in ("m1", "m2", "m3", "n1", "n2", "fin1", "fin2", "fin3"):
            steps[name + stage] = getattr(gather, stage)
    for dx in Scatter.ORDER:
        steps[f"pb{dx}"] = functools.partial(back_block, dx)
    for quarter in range(4):
        steps[f"g{quarter}"] = functools.partial(weight_grads, quarter)
    for h in range(2):
        steps[f"att{h}"] = functools.partial(attend_forward, h)
        steps[f"back{h}"] = functools.partial(attend_backward, h)
        for dx in Scatter.ORDER:
            steps[f"pf{h}{dx}"] = functools.partial(forward_block, h, dx)
        for name, sums in ((f"rf{h}", rs_f[h]), (f"rb{h}", rs_b[h])):
            for dx in Scatter.ORDER:
                steps[f"{name}j{dx}"] = functools.partial(sums.join, dx)
            for stage in "ABCDE":
                steps[name + stage] = getattr(sums, "cross_" + stage.lower())
        steps[f"rf{h}T"] = functools.partial(finish_forward, h)
        steps[f"rb{h}T"] = functools.partial(finish_back, h)

    for i, name in enumerate(SEQUENCE):
        if i == 1:
            misc.send(1, inc, parkn_out, at.relay(4))
        steps[name]()
    copies[1].start()
    copies[2].start()

    gain_sum = gain_send[at.d]
    for k in range(1, ranks):
        gains.take(k, gain_recv.at[k], (at.s, lax.rem(at.d + k, ranks)))
        gain_sum = gain_sum + gain_recv[k]
    gain_out[...] = gain_sum

    for copy in copies:
        copy.wait()
    for mover in [ag["b"].move, gains] + [sums.move for sums in rs_f + rs_b]:
        mover.drain()
    misc.take(1, parkn_out, at.relay(4))
    for i in range(2):
        misc.take(5 + i, back_out.at[pl.ds(i * 32, 32)], at.relay(1))
        misc.take(7 + i, next_out.at[:, halves[i]], at.relay(-1))
    misc.drain()


def deliver(*refs):
    count = (len(refs) - 1) // 3
    sem, held = refs[-1], refs[2 * count:3 * count]
    into = [pltpu.make_async_copy(refs[i], held[i], sem.at[i]) for i in range(count)]
    out = [pltpu.make_async_copy(held[i], refs[count + i], sem.at[count + i]) for i in range(count)]
    for copy in into:
        copy.start()
    for first, second in zip(into, out):
        first.wait()
        second.start()
    for copy in out:
        copy.wait()


def cycle(inc, parked, cot, gain, teacher, language, wq, wkv, wo):
    tokens, width = inc.shape
    ranks = lax.axis_size("dp")
    length = tokens * ranks
    any_spec = pl.BlockSpec(memory_space=pl.ANY)
    vmem_spec = pl.BlockSpec(memory_space=pltpu.VMEM)
    block = jax.ShapeDtypeStruct((tokens, width), BF16)
    shapes = [block, block, block] + [jax.ShapeDtypeStruct(w.shape, BF16) for w in (wq, wkv, wo)]
    heads_width, head_dim = wq.shape[1], wkv.shape[1]
    scratch = [
        pltpu.VMEM((3, length, width), BF16),
        pltpu.VMEM((2, Scatter.ROWS, width), BF16),
        pltpu.VMEM(wq.shape, BF16),
        pltpu.VMEM(wkv.shape, BF16),
        pltpu.VMEM(wo.shape, BF16),
        pltpu.VMEM(wo.shape, BF16),
        pltpu.VMEM((tokens, width), BF16),
        pltpu.VMEM((tokens, width), BF16),
        pltpu.VMEM((tokens, width), BF16),
        pltpu.VMEM((tokens, width), BF16),
        pltpu.VMEM((tokens, width), BF16),
        pltpu.VMEM((tokens, width), F32),
        pltpu.VMEM((2, length, heads_width), BF16),
        pltpu.VMEM((2, 2, length, head_dim), BF16),
        pltpu.VMEM((2, length, heads_width), BF16),
        pltpu.VMEM((length, heads_width), BF16),
        pltpu.VMEM((length, heads_width), BF16),
        pltpu.VMEM((length, head_dim), F32),
        pltpu.VMEM((length, head_dim), F32),
        pltpu.VMEM((length, head_dim), BF16),
        pltpu.VMEM((length, head_dim), BF16),
        pltpu.VMEM((length, head_dim), BF16),
        pltpu.VMEM((ranks, 1, width // ranks), F32),
        pltpu.VMEM((ranks, 1, width // ranks), F32),
        pltpu.SemaphoreType.DMA((3, 34)),
        pltpu.SemaphoreType.DMA((3, 34)),
        pltpu.SemaphoreType.DMA((4, 25)),
        pltpu.SemaphoreType.DMA((4, 25)),
        pltpu.SemaphoreType.DMA((9,)),
        pltpu.SemaphoreType.DMA((9,)),
        pltpu.SemaphoreType.DMA((ranks,)),
        pltpu.SemaphoreType.DMA((ranks,)),
        pltpu.SemaphoreType.DMA((8,)),
    ]
    results = pl.pallas_call(
        kernel,
        out_shape=shapes + [jax.ShapeDtypeStruct((1, width // ranks), F32)],
        in_specs=[any_spec, any_spec, any_spec, vmem_spec, vmem_spec, vmem_spec, any_spec, any_spec, any_spec],
        out_specs=[any_spec] * 6 + [vmem_spec],
        scratch_shapes=scratch,
        compiler_params=pltpu.CompilerParams(
            collective_id=0, has_side_effects=True, vmem_limit_bytes=62 * 2**20
        ),
        cost_estimate=pl.CostEstimate(flops=24 * 10**9, bytes_accessed=2 * 10**7, transcendentals=4 * 10**6),
        name="relay_cycle",
    )(inc, parked, cot, gain, teacher, language, wq, wkv, wo)
    delivered = pl.pallas_call(
        deliver,
        out_shape=shapes,
        in_specs=[any_spec] * 6,
        out_specs=[any_spec] * 6,
        scratch_shapes=[pltpu.VMEM(shape.shape, BF16) for shape in shapes] + [pltpu.SemaphoreType.DMA((12,))],
        compiler_params=pltpu.CompilerParams(vmem_limit_bytes=62 * 2**20),
        name="deliver",
    )(*results[:6])
    return (*delivered, results[6])


def body(
    incoming,
    parked,
    cotangent,
    norm_gain,
    query_weight,
    keyval_weight,
    output_weight,
    teacher_id,
    language_id,
):
    results = cycle(
        incoming[0], parked[0], cotangent[0], norm_gain, teacher_id[None], language_id[None],
        query_weight[0], keyval_weight[0], output_weight[0],
    )
    return tuple(item[None] for item in results[:6]) + (results[6],)


def solution(mesh):
    return jax.shard_map(
        body,
        mesh=mesh,
        in_specs=(
            P("section", "dp", None),
            P("section", "dp", None),
            P("section", "dp", None),
            P("section", None),
            P("section", None, "dp"),
            P("section", None, "dp"),
            P("section", "dp", None),
            P("dp"),
            P("dp"),
        ),
        out_specs=(
            P("section", "dp", None),
            P("section", "dp", None),
            P("section", "dp", None),
            P("section", None, "dp"),
            P("section", None, "dp"),
            P("section", "dp", None),
            P("section", "dp"),
        ),
        check_vma=False,
    )
```

```python
import functools
import math

import jax
import jax.numpy as jnp
from jax import lax
from jax.experimental import pallas as pl
from jax.experimental.pallas import tpu as pltpu
from jax.sharding import PartitionSpec as P

LANGS = 16
EPSILON = 1e-05
NEG_FILL = -1e30
MESH = pl.DeviceIdType.MESH
BF16 = jnp.bfloat16
F32 = jnp.float32

SHARD = 64
WHOLE = (0, 64)
PLACES = [(0, 0), (0, 1), (-1, 0), (1, 0), (2, 0), (-1, 1), (1, 1), (2, 1)]


def dot(a, b, dims=((1,), (0,))):
    return lax.dot_general(a, b, (dims, ((), ())), preferred_element_type=F32)


class Split:
    def __init__(self, low, a_cut, middle, b_cut, high):
        self.whole = (low, high - low)
        self.A, self.A0, self.A1 = (low, middle - low), (low, a_cut - low), (a_cut, middle - a_cut)
        self.B, self.B0, self.B1 = (middle, high - middle), (middle, b_cut - middle), (b_cut, high - b_cut)


EVEN = Split(0, 16, 32, 48, 64)
TILT_RIGHT = Split(0, 16, 16, 32, 64)
TILT_LEFT = Split(0, 0, 16, 48, 64)
UPPER = Split(0, 16, 16, 16, 32)
LOWER = Split(32, 32, 48, 64, 64)


SEQUENCE = [
    "fs", "fm1", "fm2", "bs", "ffin1", "fm3", "fn1", "fn2", "us", "bm1", "ffin2", "ffin3", "um1", "bm3",
    "bm2", "projf", "att0", "att1", "pf00", "bfin1", "bn1", "um2", "rf0j0", "pf02", "un1", "pf01", "pf10",
    "um3", "rf0j2", "pf1-1", "pf11", "bn2", "pf0-1", "ufin1", "rf1j0", "pf12", "bfin2", "un2", "rf0j-1",
    "bfin3", "projb", "rf1j1", "rf0j1", "ufin2", "rf1j2", "rf0B", "rf1j-1", "ufin3", "cot", "rf1B", "rf0A",
    "back0", "rf0D", "rf0C", "back1", "rf0E", "dkv", "rf1D", "og", "rf0T", "dkvt", "pb2", "pb-1", "rf1C",
    "rb0j2", "pb1", "rb0j-1", "rf1A", "pb0", "rb0j1", "rb0B", "rb0j0", "rb1j0", "rb0A", "g1", "rb1j2", "rb0C",
    "rb1j-1", "rb1A", "rb1j1", "rb1B", "rf1E", "g0", "rb0D", "rb0E", "rb1D", "g3", "rb1E", "rf1T", "rb0T",
    "g2", "rb1C", "rb1T",
]
GATHER_SPLITS = (EVEN, EVEN, TILT_LEFT)
SCATTER_SPLITS = (TILT_LEFT, EVEN)


class Place:
    def __init__(self):
        self.s = lax.axis_index("section")
        self.d = lax.axis_index("dp")
        self.x = self.d // 4
        self.y = lax.rem(self.d // 2, 2)
        self.c = lax.rem(self.d, 2)

    def index(self, dx, dy, flip=0):
        x = lax.rem(self.x + dx + 4, 4)
        y = self.y if dy == 0 else 1 - self.y
        c = self.c if flip == 0 else 1 - self.c
        return x * 4 + y * 2 + c

    def row(self, dx, dy, part, flip=0):
        start = self.index(dx, dy, flip) * SHARD + part[0]
        return pl.ds(pl.multiple_of(start, 16), part[1])

    def peer(self, dx, dy, flip=0):
        return (self.s, self.index(dx, dy, flip))

    def relay(self, steps):
        return (lax.rem(self.s + steps + 8, 8), self.d)


class Mover:
    def __init__(self, send_sem, recv_sem):
        self.send_sem, self.recv_sem = send_sem, recv_sem
        self.open = []

    def send(self, key, src, dst, target):
        copy = pltpu.make_async_remote_copy(
            src_ref=src, dst_ref=dst, send_sem=self.send_sem.at[key], recv_sem=self.recv_sem.at[key],
            device_id=target, device_id_type=MESH,
        )
        copy.start()
        self.open.append(copy)

    def take(self, key, dst, source):
        pltpu.make_async_remote_copy(
            src_ref=dst, dst_ref=dst, send_sem=self.send_sem.at[key], recv_sem=self.recv_sem.at[key],
            device_id=source, device_id_type=MESH,
        ).wait_recv()

    def drain(self):
        for copy in self.open:
            copy.wait_send()
        self.open = []


class Gather:
    def __init__(self, place, split, buf, send_sem, recv_sem):
        self.at, self.split, self.buf = place, split, buf
        self.move = Mover(send_sem, recv_sem)

    def go(self, key, where, part, to):
        if part[1]:
            rows = self.buf.at[self.at.row(*where, part)]
            self.move.send(key, rows, rows, self.at.peer(*to))

    def sib(self, where, part):
        key = 18 + 2 * PLACES.index(where) + (0 if part == self.split.A else 1)
        rows = self.buf.at[self.at.row(*where, part)]
        self.move.send(key, rows, rows, self.at.peer(0, 0, 1))

    def got(self, key, where, part):
        if part[1]:
            self.move.take(key, self.buf.at[self.at.row(*where, part)], self.at.peer(0, 1))

    def start(self):
        own, right, left, up = (0, 0), (1, 0), (-1, 0), (0, 1)
        self.go(13, own, self.split.B, up)
        self.go(0, own, self.split.A, right)
        self.go(6, own, self.split.A, left)
        self.go(12, own, self.split.A, up)
        self.go(1, own, self.split.B, right)
        self.go(7, own, self.split.B, left)
        self.sib(own, self.split.A)
        self.sib(own, self.split.B)

    def m1(self):
        self.got(13, (0, 1), self.split.B)
        self.go(2, (0, 1), self.split.B, (1, 0))
        self.go(8, (0, 1), self.split.B, (-1, 0))
        self.sib((0, 1), self.split.B)

    def m2(self):
        self.got(0, (-1, 0), self.split.A)
        self.go(3, (-1, 0), self.split.A0, (1, 0))
        self.go(14, (-1, 0), self.split.A, (0, 1))
        self.got(6, (1, 0), self.split.A)
        self.go(9, (1, 0), self.split.A1, (-1, 0))
        self.go(15, (1, 0), self.split.A, (0, 1))
        self.sib((-1, 0), self.split.A)
        self.sib((1, 0), self.split.A)

    def m3(self):
        self.got(1, (-1, 0), self.split.B)
        self.go(4, (-1, 0), self.split.B0, (1, 0))
        self.got(7, (1, 0), self.split.B)
        self.go(10, (1, 0), self.split.B1, (-1, 0))
        self.sib((-1, 0), self.split.B)
        self.sib((1, 0), self.split.B)

    def n1(self):
        self.got(2, (-1, 1), self.split.B)
        self.go(5, (-1, 1), self.split.B0, (1, 0))
        self.got(8, (1, 1), self.split.B)
        self.go(11, (1, 1), self.split.B1, (-1, 0))
        self.sib((-1, 1), self.split.B)
        self.sib((1, 1), self.split.B)

    def n2(self):
        self.got(3, (2, 0), self.split.A0)
        self.got(9, (2, 0), self.split.A1)
        self.go(16, (2, 0), self.split.A, (0, 1))
        self.sib((2, 0), self.split.A)

    def fin1(self):
        for key, where in ((12, (0, 1)), (14, (-1, 1)), (15, (1, 1))):
            self.got(key, where, self.split.A)
            self.sib(where, self.split.A)

    def fin2(self):
        self.got(4, (2, 0), self.split.B0)
        self.got(10, (2, 0), self.split.B1)
        self.sib((2, 0), self.split.B)
        self.got(5, (2, 1), self.split.B0)
        self.got(11, (2, 1), self.split.B1)
        self.sib((2, 1), self.split.B)
        self.got(16, (2, 1), self.split.A)
        self.sib((2, 1), self.split.A)

    def fin3(self):
        for i, where in enumerate(PLACES):
            for j, part in enumerate((self.split.A, self.split.B)):
                self.move.take(18 + 2 * i + j, self.buf.at[self.at.row(*where, part, 1)], self.at.peer(0, 0, 1))


class Scatter:
    ORDER = [2, 1, -1, 0]
    ROWS = 7 * SHARD + 8 * SHARD

    def __init__(self, place, split, buf, land, base, cols, send_sem, recv_sem):
        self.at, self.split, self.buf, self.land, self.cols = place, split, buf, land, cols
        self.move = Mover(send_sem, recv_sem)
        p = split
        parts = [p.B0, p.B0, p.A0, p.B, p.B, p.A, p.B1, p.B1, p.A1, p.B, p.B, p.A, p.A, p.A, p.A, p.A, p.B] + [p.whole] * 8
        self.sizes = [part[1] for part in parts]
        self.offsets = [base + sum(self.sizes[:i]) for i in range(len(parts))]

    def slot(self, key):
        return self.land.at[pl.ds(self.offsets[key], self.sizes[key]), self.cols]

    def go(self, key, where, part, to):
        if part[1]:
            rows = self.buf.at[self.at.row(*where, part), self.cols]
            self.move.send(key, rows, self.slot(key), self.at.peer(*to))

    def add(self, key, where, part):
        if part[1]:
            self.move.take(key, self.slot(key), self.at.peer(0, 1))
            rows = self.at.row(*where, part)
            total = self.buf[rows, self.cols].astype(F32) + self.slot(key)[...].astype(F32)
            self.buf[rows, self.cols] = total.astype(BF16)

    def block(self, dx):
        return pl.multiple_of(lax.rem(self.at.x + dx + 4, 4) * 256, 256)

    def share(self, dx):
        for dy in (1, 0):
            key = 17 + 2 * self.ORDER.index(dx) + dy
            rows = self.buf.at[self.at.row(dx, dy, self.split.whole, 1), self.cols]
            self.move.send(key, rows, self.slot(key), self.at.peer(0, 0, 1))

    def join(self, dx):
        right, left, up = (1, 0), (-1, 0), (0, 1)
        for dy in (1, 0):
            self.add(17 + 2 * self.ORDER.index(dx) + dy, (dx, dy), self.split.whole)
        if dx == 2:
            self.go(0, (2, 1), self.split.B0, left)
            self.go(6, (2, 1), self.split.B1, right)
            self.go(12, (2, 1), self.split.A, up)
            self.go(1, (2, 0), self.split.B0, left)
            self.go(7, (2, 0), self.split.B1, right)
        else:
            self.go({-1: 13, 1: 14, 0: 15}[dx], (dx, 1), self.split.A, up)

    def cross_a(self):
        self.add(12, (2, 0), self.split.A)
        self.go(2, (2, 0), self.split.A0, (-1, 0))
        self.go(8, (2, 0), self.split.A1, (1, 0))

    def cross_b(self):
        self.add(0, (-1, 1), self.split.B0)
        self.go(3, (-1, 1), self.split.B, (-1, 0))
        self.add(6, (1, 1), self.split.B1)
        self.go(9, (1, 1), self.split.B, (1, 0))

    def cross_c(self):
        self.add(1, (-1, 0), self.split.B0)
        self.go(4, (-1, 0), self.split.B, (-1, 0))
        self.add(7, (1, 0), self.split.B1)
        self.go(10, (1, 0), self.split.B, (1, 0))

    def cross_d(self):
        self.add(3, (0, 1), self.split.B)
        self.add(9, (0, 1), self.split.B)
        self.go(16, (0, 1), self.split.B, (0, 1))

    def cross_e(self):
        self.add(13, (-1, 0), self.split.A)
        self.add(2, (-1, 0), self.split.A0)
        self.go(5, (-1, 0), self.split.A, (-1, 0))
        self.add(14, (1, 0), self.split.A)
        self.add(8, (1, 0), self.split.A1)
        self.go(11, (1, 0), self.split.A, (1, 0))

    def total(self, out, start=None):
        for part, keys in ((self.split.A, (15, 5, 11)), (self.split.B, (4, 10, 16))):
            rows = pl.ds(*part)
            whole = self.buf[self.at.row(0, 0, part), self.cols].astype(F32)
            for key in keys:
                self.move.take(key, self.slot(key), self.at.peer(0, 1))
                whole = whole + self.slot(key)[...].astype(F32)
            if start is not None:
                whole = whole + start[rows, self.cols].astype(F32)
            out[rows, self.cols] = whole.astype(out.dtype)


def softmax_block(q_blk, keys, first):
    rows, length = q_blk.shape[0], keys.shape[0]
    scale = 1.0 / math.sqrt(q_blk.shape[1])
    scores = dot(q_blk, keys, ((1,), (1,)))
    row_index = lax.broadcasted_iota(jnp.int32, (rows, length), 0) + first
    col_index = lax.broadcasted_iota(jnp.int32, (rows, length), 1)
    scores = jnp.where(col_index <= row_index, scores, NEG_FILL)
    weights = jnp.exp((scores - jnp.max(scores, axis=-1, keepdims=True)) * scale)
    return weights, jnp.sum(weights, axis=-1, keepdims=True)


def kernel(
    inc_hbm, parked, cot_hbm, gain, teacher, language, wq_hbm, wkv_hbm, wo_hbm,
    next_out, back_out, parkn_out, qg_out, kg_out, og_out, gain_out,
    g, land, wq, wkv, wo, og, inc, cot, stash, fwd_rows, back_rows, d_rows, q, kv, att, d_out, dq, dk, dv,
    dkv_send, dkv_recv, dkv, gain_send, gain_recv,
    ag_send, ag_recv, rs_send, rs_recv, misc_send, misc_recv, gs_send, gs_recv, local_sem,
):
    at = Place()
    length, width = g.shape[1], g.shape[2]
    blocks, ranks = length // 256, length // SHARD

    loads = [
        pltpu.make_async_copy(src, dst, local_sem.at[i])
        for i, (src, dst) in enumerate(
            ((inc_hbm, inc), (cot_hbm, cot), (wq_hbm, wq), (wkv_hbm, wkv), (wo_hbm, wo))
        )
    ]
    for load in loads:
        load.start()
    barrier = pltpu.get_barrier_semaphore()
    peers = [(at.s, lax.rem(at.d + k, ranks)) for k in range(1, ranks)] + [at.relay(4), at.relay(1), at.relay(-1)]
    for peer in peers:
        pl.semaphore_signal(barrier, inc=1, device_id=peer, device_id_type=MESH)

    own = at.row(0, 0, WHOLE)
    core = at.c

    def inverse_rms(values):
        return lax.rsqrt(jnp.mean(values * values, axis=-1, keepdims=True) + EPSILON)

    def normalized(rows):
        values = rows[...].astype(F32)
        return (values * inverse_rms(values) * gain[...]).astype(BF16)

    weight = jnp.exp2(-teacher[...].astype(F32)) * (0.5 + language[...].astype(F32) / (LANGS - 1))
    weight = jnp.where(at.s == lax.axis_size("section") - 1, weight, 1.0)
    square = lax.broadcasted_iota(jnp.int32, (SHARD, SHARD), 0) == lax.broadcasted_iota(jnp.int32, (SHARD, SHARD), 1)
    weight = jnp.sum(jnp.where(square, weight, 0.0), axis=1, keepdims=True)
    loads[0].wait()
    g[0, own, :] = normalized(inc)

    pl.semaphore_wait(barrier, len(peers))
    misc = Mover(misc_send, misc_recv)
    misc.send(0, parked, stash, at.relay(4))
    ag = {
        name: Gather(at, split, g.at[i], ag_send.at[i], ag_recv.at[i])
        for i, (name, split) in enumerate(zip("fub", GATHER_SPLITS))
    }
    loaded = set()

    def loads_done(*names):
        for name in names:
            if name not in loaded:
                loaded.add(name)
                loads[name].wait()

    def start_u():
        loads_done(1)
        cot[...] = (cot[...].astype(F32) * weight).astype(BF16)
        g[1, own, :] = cot[...]
        ag["u"].start()

    def start_b():
        misc.take(0, stash, at.relay(4))
        g[2, own, :] = normalized(stash)
        ag["b"].start()

    def project(source, slot):
        loads_done(2, 3)

        def step(i, carry):
            rows = pl.ds(pl.multiple_of(i * 256, 256), 256)
            piece = g[source, rows, :]
            q[slot, rows, :] = dot(piece, wq[...]).astype(BF16)
            kv[slot, core, rows, :] = dot(piece, wkv[...]).astype(BF16)
            return carry

        lax.fori_loop(0, blocks, step, 0)
        misc.send(2 + slot, kv.at[slot, core], kv.at[slot, core], at.peer(0, 0, 1))

    def keyval_arrived(slot):
        misc.take(2 + slot, kv.at[slot, 1 - core], at.peer(0, 0, 1))

    def attend(head):
        cols = pl.ds(head * 128, 128)
        for i in range(blocks):
            rows, seen = pl.ds(i * 256, 256), pl.ds(0, (i + 1) * 256)
            weights, norm = softmax_block(q[0, rows, cols], kv[0, 0, seen, :], i * 256)
            att[0, rows, cols] = (dot(weights.astype(BF16), kv[0, 1, seen, :]) / norm).astype(BF16)

    def attend_back(head):
        cols = pl.ds(head * 128, 128)
        for i in range(blocks):
            rows, seen = pl.ds(i * 256, 256), pl.ds(0, (i + 1) * 256)
            q_blk, keys, vals = q[1, rows, cols], kv[1, 0, seen, :], kv[1, 1, seen, :]
            weights, norm = softmax_block(q_blk, keys, i * 256)
            weights = weights / norm
            rounded = weights.astype(BF16)
            att[1, rows, cols] = dot(rounded, vals).astype(BF16)
            d_blk = d_out[rows, cols]
            d_weights = dot(d_blk, vals, ((1,), (1,)))
            delta = jnp.sum(weights * d_weights, axis=-1, keepdims=True)
            d_scores = (weights * (d_weights - delta) * scale).astype(BF16)
            dq[rows, cols] = dot(d_scores, keys).astype(BF16)
            dk[seen, :] += dot(d_scores, q_blk, ((0,), (0,)))
            dv[seen, :] += dot(rounded, d_blk, ((0,), (0,)))

    half = width // 2
    halves = [pl.ds(0, half), pl.ds(half, half)]
    rows_of = Scatter.ROWS // 2
    rs_f = [
        Scatter(at, split, g.at[0], land.at[0], 0, halves[h], rs_send.at[h], rs_recv.at[h])
        for h, split in enumerate(SCATTER_SPLITS)
    ]
    rs_b = [
        Scatter(at, split, g.at[1], land.at[1], h * rows_of, pl.ds(0, width), rs_send.at[2 + h], rs_recv.at[2 + h])
        for h, split in enumerate((UPPER, LOWER))
    ]

    def produce(dx, buf, first, count, term):
        rows = pl.ds(rs_f[0].block(dx), 256)

        def step(j, carry):
            cols = pl.ds(pl.multiple_of(first + j * 1024, 1024), 1024)
            g[buf, rows, cols] = term(rows, cols).astype(BF16)
            return carry

        lax.fori_loop(0, count // 1024, step, 0)

    def forward_term(rows, cols):
        return dot(att[0, rows, :], wo[:, cols])

    def back_term(rows, cols):
        term = dot(dq[rows, :], wq[cols, :], ((1,), (1,)))
        return term + dot(dkv[rows, :], wkv[cols, :], ((1,), (1,)))

    def cotangent():
        loads_done(4)

        def step(i, carry):
            rows = pl.ds(pl.multiple_of(i * 256, 256), 256)
            d_out[rows, :] = dot(g[1, rows, :], wo[...], ((1,), (1,))).astype(BF16)
            return carry

        lax.fori_loop(0, blocks, step, 0)

    arrived = set()

    def once(key, act):
        if key not in arrived:
            arrived.add(key)
            act()

    def attend_forward(head):
        once("keyval f", lambda: keyval_arrived(0))
        attend(head)

    def attend_backward(head):
        if head == 0:
            dk[...] = jnp.zeros_like(dk)
            dv[...] = jnp.zeros_like(dv)
            keyval_arrived(1)
        attend_back(head)

    scale = 1.0 / math.sqrt(dk.shape[1])
    even = core == 0

    def swap_keyval():
        dkv_send[...] = jnp.where(even, dv[...], dk[...]).astype(BF16)
        misc.send(4, dkv_send, dkv_recv, at.peer(0, 0, 1))

    def take_keyval():
        misc.take(4, dkv_recv, at.peer(0, 0, 1))
        dkv[...] = (jnp.where(even, dk[...], dv[...]) + dkv_recv[...].astype(F32)).astype(BF16)

    def output_grad():
        att_t = att[1].T

        def step(j, carry):
            cols = pl.ds(pl.multiple_of(j * 512, 512), 512)
            og[:, cols] = dot(att_t, g[1, :, cols]).astype(BF16)
            return carry

        lax.fori_loop(0, width // 512, step, 0)
        copies[0].start()

    def forward_block(h, dx):
        once("drain f", ag["f"].move.drain)
        loads_done(4)
        produce(dx, 0, h * half, half, forward_term)
        rs_f[h].share(dx)

    def back_block(dx):
        once("drain u", ag["u"].move.drain)
        produce(dx, 1, 0, width, back_term)
        for sums in rs_b:
            sums.share(dx)

    def weight_grads(quarter):
        grad_t = jnp.concatenate([dq[...], dkv[...]], axis=1).T

        def step(j, carry):
            cols = pl.ds(pl.multiple_of(j * 512, 512), 512)
            block = dot(grad_t, g[2, :, cols]).astype(BF16).T
            wq[cols, :] = block[:, :256]
            wkv[cols, :] = block[:, 256:]
            return carry

        steps = width // 2048
        lax.fori_loop(quarter * steps, (quarter + 1) * steps, step, 0)

    def finish_forward(h):
        rs_f[h].total(fwd_rows, inc)
        misc.send(7 + h, fwd_rows.at[:, halves[h]], next_out.at[:, halves[h]], at.relay(1))

    gain_parts = []

    def finish_back(h):
        rs_b[h].total(d_rows)
        rows = pl.ds(h * 32, 32)
        d_normed = d_rows[rows, :]
        values = stash[rows, :].astype(F32)
        inverse = inverse_rms(values)
        scaled = d_normed * gain[...]
        inner = jnp.mean(scaled * values, axis=-1, keepdims=True)
        change = inverse * scaled - values * (inverse * inverse * inverse * inner)
        back_rows[rows, :] = (cot[rows, :].astype(F32) + change).astype(BF16)
        misc.send(5 + h, back_rows.at[rows], back_out.at[rows], at.relay(-1))
        gain_parts.append(jnp.sum(d_normed * (values * inverse), axis=0, keepdims=True))
        if len(gain_parts) == 2:
            d_gain = gain_parts[0] + gain_parts[1]
            for k in range(ranks):
                gain_send[k] = d_gain[:, k * piece:(k + 1) * piece]
            for k in range(1, ranks):
                there = lax.rem(at.d + k, ranks)
                gains.send(k, gain_send.at[there], gain_recv.at[k], (at.s, there))

    gains = Mover(gs_send, gs_recv)
    piece = width // ranks
    copies = [
        pltpu.make_async_copy(src, dst, local_sem.at[5 + i])
        for i, (src, dst) in enumerate(((og, og_out), (wq, qg_out), (wkv, kg_out)))
    ]

    steps = {
        "fs": ag["f"].start, "us": start_u, "bs": start_b,
        "projf": lambda: project(0, 0), "projb": lambda: project(2, 1), "cot": cotangent,
        "dkv": swap_keyval, "dkvt": take_keyval, "og": output_grad,
    }
    for name, gather in ag.items():
        for stage in ("m1", "m2", "m3", "n1", "n2", "fin1", "fin2", "fin3"):
            steps[name + stage] = getattr(gather, stage)
    for dx in Scatter.ORDER:
        steps[f"pb{dx}"] = functools.partial(back_block, dx)
    for quarter in range(4):
        steps[f"g{quarter}"] = functools.partial(weight_grads, quarter)
    for h in range(2):
        steps[f"att{h}"] = functools.partial(attend_forward, h)
        steps[f"back{h}"] = functools.partial(attend_backward, h)
        for dx in Scatter.ORDER:
            steps[f"pf{h}{dx}"] = functools.partial(forward_block, h, dx)
        for name, sums in ((f"rf{h}", rs_f[h]), (f"rb{h}", rs_b[h])):
            for dx in Scatter.ORDER:
                steps[f"{name}j{dx}"] = functools.partial(sums.join, dx)
            for stage in "ABCDE":
                steps[name + stage] = getattr(sums, "cross_" + stage.lower())
        steps[f"rf{h}T"] = functools.partial(finish_forward, h)
        steps[f"rb{h}T"] = functools.partial(finish_back, h)

    for i, name in enumerate(SEQUENCE):
        if i == 1:
            misc.send(1, inc, parkn_out, at.relay(4))
        steps[name]()
    copies[1].start()
    copies[2].start()

    gain_sum = gain_send[at.d]
    for k in range(1, ranks):
        gains.take(k, gain_recv.at[k], (at.s, lax.rem(at.d + k, ranks)))
        gain_sum = gain_sum + gain_recv[k]
    gain_out[...] = gain_sum

    for copy in copies:
        copy.wait()
    for mover in [ag["b"].move, gains] + [sums.move for sums in rs_f + rs_b]:
        mover.drain()
    misc.take(1, parkn_out, at.relay(4))
    for i in range(2):
        misc.take(5 + i, back_out.at[pl.ds(i * 32, 32)], at.relay(1))
        misc.take(7 + i, next_out.at[:, halves[i]], at.relay(-1))
    misc.drain()


def deliver(*refs):
    count = (len(refs) - 1) // 3
    sem, held = refs[-1], refs[2 * count:3 * count]
    into, out = [], []
    for i in range(count):
        size = held[i].shape[0] // 4
        for part in range(4):
            rows, key = pl.ds(part * size, size), 4 * i + part
            into.append(pltpu.make_async_copy(refs[i].at[rows], held[i].at[rows], sem.at[0, key]))
            out.append(pltpu.make_async_copy(held[i].at[rows], refs[count + i].at[rows], sem.at[1, key]))
    for copy in into:
        copy.start()
    for first, second in zip(into, out):
        first.wait()
        second.start()
    for copy in out:
        copy.wait()


def cycle(inc, parked, cot, gain, teacher, language, wq, wkv, wo):
    tokens, width = inc.shape
    ranks = lax.axis_size("dp")
    length = tokens * ranks
    any_spec = pl.BlockSpec(memory_space=pl.ANY)
    vmem_spec = pl.BlockSpec(memory_space=pltpu.VMEM)
    block = jax.ShapeDtypeStruct((tokens, width), BF16)
    shapes = [block, block, block] + [jax.ShapeDtypeStruct(w.shape, BF16) for w in (wq, wkv, wo)]
    heads_width, head_dim = wq.shape[1], wkv.shape[1]
    scratch = [
        pltpu.VMEM((3, length, width), BF16),
        pltpu.VMEM((2, Scatter.ROWS, width), BF16),
        pltpu.VMEM(wq.shape, BF16),
        pltpu.VMEM(wkv.shape, BF16),
        pltpu.VMEM(wo.shape, BF16),
        pltpu.VMEM(wo.shape, BF16),
        pltpu.VMEM((tokens, width), BF16),
        pltpu.VMEM((tokens, width), BF16),
        pltpu.VMEM((tokens, width), BF16),
        pltpu.VMEM((tokens, width), BF16),
        pltpu.VMEM((tokens, width), BF16),
        pltpu.VMEM((tokens, width), F32),
        pltpu.VMEM((2, length, heads_width), BF16),
        pltpu.VMEM((2, 2, length, head_dim), BF16),
        pltpu.VMEM((2, length, heads_width), BF16),
        pltpu.VMEM((length, heads_width), BF16),
        pltpu.VMEM((length, heads_width), BF16),
        pltpu.VMEM((length, head_dim), F32),
        pltpu.VMEM((length, head_dim), F32),
        pltpu.VMEM((length, head_dim), BF16),
        pltpu.VMEM((length, head_dim), BF16),
        pltpu.VMEM((length, head_dim), BF16),
        pltpu.VMEM((ranks, 1, width // ranks), F32),
        pltpu.VMEM((ranks, 1, width // ranks), F32),
        pltpu.SemaphoreType.DMA((3, 34)),
        pltpu.SemaphoreType.DMA((3, 34)),
        pltpu.SemaphoreType.DMA((4, 25)),
        pltpu.SemaphoreType.DMA((4, 25)),
        pltpu.SemaphoreType.DMA((9,)),
        pltpu.SemaphoreType.DMA((9,)),
        pltpu.SemaphoreType.DMA((ranks,)),
        pltpu.SemaphoreType.DMA((ranks,)),
        pltpu.SemaphoreType.DMA((8,)),
    ]
    results = pl.pallas_call(
        kernel,
        out_shape=shapes + [jax.ShapeDtypeStruct((1, width // ranks), F32)],
        in_specs=[any_spec, any_spec, any_spec, vmem_spec, vmem_spec, vmem_spec, any_spec, any_spec, any_spec],
        out_specs=[any_spec] * 6 + [vmem_spec],
        scratch_shapes=scratch,
        compiler_params=pltpu.CompilerParams(
            collective_id=0, has_side_effects=True, vmem_limit_bytes=62 * 2**20
        ),
        cost_estimate=pl.CostEstimate(flops=24 * 10**9, bytes_accessed=2 * 10**7, transcendentals=4 * 10**6),
        name="relay_cycle",
    )(inc, parked, cot, gain, teacher, language, wq, wkv, wo)
    delivered = pl.pallas_call(
        deliver,
        out_shape=shapes,
        in_specs=[any_spec] * 6,
        out_specs=[any_spec] * 6,
        scratch_shapes=[pltpu.VMEM(shape.shape, BF16) for shape in shapes] + [pltpu.SemaphoreType.DMA((2, 24))],
        compiler_params=pltpu.CompilerParams(vmem_limit_bytes=62 * 2**20),
        name="deliver",
    )(*results[:6])
    return (*delivered, results[6])


def body(
    incoming,
    parked,
    cotangent,
    norm_gain,
    query_weight,
    keyval_weight,
    output_weight,
    teacher_id,
    language_id,
):
    results = cycle(
        incoming[0], parked[0], cotangent[0], norm_gain, teacher_id[None], language_id[None],
        query_weight[0], keyval_weight[0], output_weight[0],
    )
    return tuple(item[None] for item in results[:6]) + (results[6],)


def solution(mesh):
    return jax.shard_map(
        body,
        mesh=mesh,
        in_specs=(
            P("section", "dp", None),
            P("section", "dp", None),
            P("section", "dp", None),
            P("section", None),
            P("section", None, "dp"),
            P("section", None, "dp"),
            P("section", "dp", None),
            P("dp"),
            P("dp"),
        ),
        out_specs=(
            P("section", "dp", None),
            P("section", "dp", None),
            P("section", "dp", None),
            P("section", None, "dp"),
            P("section", None, "dp"),
            P("section", "dp", None),
            P("section", "dp"),
        ),
        check_vma=False,
    )
```
